128 devices in a mesh: dp: 64 (over y, z_hi, x, core), tensor: 2 (over z_lo).
Axes of the slice: x: 4, y: 4, z: 4 (z_hi: 2, z_lo: 2; z = z_hi * 2 + z_lo), core: 2. Of those that a mesh axis runs over, the one named last changes fastest.
Arguments:
- tokens: bfloat16 [64, 1024, 768], P('dp'), may hold values from -6 to 6
- segment_ids: int32 [64, 1024], P('dp'), may hold values from 0 to 2, never falling along the last dimension, each value on 1 to 512 neighbouring positions
- norm_gain: bfloat16 [768], replicated, may hold values from 0.25 to 1.75
- proj_main: bfloat16 [768, 2, 1536], P(None, None, 'tensor'), may hold values from -0.21875 to 0.21875
- proj_state: bfloat16 [768, 256], replicated, may hold values from -0.21875 to 0.21875
- proj_step: bfloat16 [768, 24], P(None, 'tensor'), may hold values from -0.21875 to 0.21875
- conv_main: float32 [4, 1536], P(None, 'tensor'), may hold values from -3 to 3
- conv_state: float32 [4, 256], replicated, may hold values from -3 to 3
- bias_main: float32 [1536], P('tensor'), may hold values from -0.5 to 0.5
- bias_state: float32 [256], replicated, may hold values from -0.5 to 0.5
- step_bias: float32 [24], P('tensor'), may hold values from -6 to -3
- log_rate: float32 [24], P('tensor'), may hold values from -1.5 to 1
- skip_gain: float32 [24], P('tensor'), may hold values from 0.5 to 1.5
- gate_gain: bfloat16 [1536], P('tensor'), may hold values from 0.25 to 1.75
- out_proj: bfloat16 [1536, 768], P('tensor'), may hold values from -0.15625 to 0.15625
- cotangent: bfloat16 [64, 1024, 768], P('dp'), may hold values from -6 to 6
Outputs:
- mixed: bfloat16 [64, 1024, 768], P('dp')
- grad_tokens: bfloat16 [64, 1024, 768], P('dp')
- grad_normgain: float32 [768], replicated
- grad_projmain: float32 [768, 2, 1536], P('dp', None, 'tensor')
- grad_projstate: float32 [768, 256], P('dp')
- grad_projstep: float32 [768, 24], P('dp', 'tensor')
- grad_convmain: float32 [4, 1536], P(None, 'tensor')
- grad_convstate: float32 [4, 256], replicated
- grad_biasmain: float32 [1536], P('tensor')
- grad_biasstate: float32 [256], replicated
- grad_stepbias: float32 [24], P('tensor')
- grad_lograte: float32 [24], P('tensor')
- grad_skipgain: float32 [24], P('tensor')
- grad_gategain: float32 [1536], P('tensor')
- grad_outproj: float32 [1536, 768], P('tensor', 'dp')
The draws below stay inside these ranges and needn't reach their ends.
Inputs may be any that keep to these rules, and one draw needn't show every extreme that they name: `segment_ids`: in each packed row the sequence numbers start at 0, never fall, and each of the 3 sequences covers 1 to 512 consecutive tokens.
All inputs are finite; a program needn't handle non-finite values.
Results may differ from the reference program's by a relative error of at most 0.012.
Values sent between devices are 32-bit elements; how exact they have to be, the bound alone decides.
No kernel may reach another device: no remote copies, remote signals or barrier semaphores. Data moves between devices by JAX's collectives and lax.ppermute only.
A program may use at most 192 MiB of HBM per device.

```python
import math
import jax
import jax.numpy as jnp
import numpy as np
from jax import lax

D = 768
INNER = 1536
STATE = 128
CONV = 4
GROUP = 256
SEGMENTS = 3
PACK_LEN = 1024
HEADS = 24
PACKS = 64


def level_of(stream_key, extent, cuts, low, largest):
    loudness = 1.0
    for position, blocks in cuts:
        steps = jax.random.uniform(jax.random.fold_in(jax.random.fold_in(stream_key, 6), position), (blocks,), jnp.float32, low / len(cuts), largest / len(cuts))
        loudness = loudness * jnp.repeat(jnp.exp(steps), extent[position] // blocks).reshape((-1,) + (1,) * (len(extent) - 1 - position))
    return loudness


def split_up(count, total, reach, slope):
    portions = [(1 << 20) // math.isqrt(rank ** slope) + 1 for rank in range(2, count + 1)]
    surplus, given = total - reach - (count - 1), [1] * (count - 1)
    while surplus > 0:
        free = [i for i in range(count - 1) if given[i] < reach]
        mass, remaining = sum([portions[i] for i in free]), surplus
        for i in free:
            more = min(reach - given[i], max(1, remaining * portions[i] // mass), surplus)
            given[i] = given[i] + more
            surplus = surplus - more
    return np.array([reach] + given)


def ragged_sizes(rng, count, total, bound, lean):
    if count == 2:
        one = jax.random.randint(rng, (), max(1, total - bound), min(bound, total - 1) + 1)
        return jnp.stack([one, total - one])
    lengths = jnp.asarray(split_up(count, total, bound, lean), jnp.int32)
    pairs = (count - 1) // 2
    giver, receiver = lengths[1:1 + 2 * pairs:2], lengths[2:2 + 2 * pairs:2]
    margin = jnp.minimum(giver - 1, bound - receiver)
    shifted = jax.random.randint(jax.random.fold_in(rng, 1), (pairs,), 0, 1 << 20) % (margin + 1)
    lengths = lengths.at[1:1 + 2 * pairs:2].set(giver - shifted).at[2:2 + 2 * pairs:2].set(receiver + shifted)
    return lengths[jax.random.permutation(jax.random.fold_in(rng, 2), count)]


def noise(rng, shape, width, bound, shards=(), dtype=jnp.bfloat16):
    result = width * jax.random.normal(rng, shape, jnp.float32)
    if shards:
        result = result * level_of(rng, shape, shards, -0.22, 0.18)
    return jnp.clip(result, -bound, bound).astype(dtype)


def setup_inputs(seed: int = 0) -> dict:
    key_of = jax.random.split(jax.random.key(seed), 17)
    return {
        "tokens": noise(key_of[0], (PACKS, PACK_LEN, D), 1.0, 6.0, ((0, 64),)),
        "segment_ids": jax.vmap(lambda own: jnp.searchsorted(jnp.cumsum(ragged_sizes(own, SEGMENTS, PACK_LEN, PACK_LEN // 2, 0)), jnp.arange(PACK_LEN), side="right"))(jax.random.split(key_of[1], PACKS)).reshape((PACKS, PACK_LEN)).astype(jnp.int32),
        "norm_gain": jnp.clip(1.0 + 0.15 * jax.random.normal(key_of[2], (D,), jnp.float32), 0.25, 1.75).astype(jnp.bfloat16),
        "proj_main": noise(key_of[3], (D, 2, INNER), D ** -0.5, 0.21875, ((2, 2),)),
        "proj_state": noise(key_of[4], (D, 2 * STATE), D ** -0.5, 0.21875),
        "proj_step": noise(key_of[5], (D, HEADS), D ** -0.5, 0.21875, ((1, 2),)),
        "conv_main": noise(key_of[6], (CONV, INNER), 0.5, 3.0, ((1, 2),), jnp.float32),
        "conv_state": noise(key_of[7], (CONV, 2 * STATE), 0.5, 3.0, (), jnp.float32),
        "bias_main": jnp.clip(jax.random.uniform(key_of[8], (INNER,), jnp.float32, -0.5, 0.5) * level_of(key_of[8], (INNER,), ((0, 2),), -0.4, 0.0), -0.5, 0.5),
        "bias_state": jnp.clip(jax.random.uniform(key_of[9], (2 * STATE,), jnp.float32, -0.5, 0.5), -0.5, 0.5),
        "step_bias": jnp.clip(-6.0 + 3.0 * jax.random.uniform(key_of[10], (HEADS,), jnp.float32) ** level_of(key_of[10], (HEADS,), ((0, 2),), -0.2, 0.2), -6.0, -3.0),
        "log_rate": jnp.clip(-1.5 + 2.5 * jax.random.uniform(key_of[11], (HEADS,), jnp.float32) ** level_of(key_of[11], (HEADS,), ((0, 2),), -0.2, 0.2), -1.5, 1.0),
        "skip_gain": jnp.clip(0.5 + 1.0 * jax.random.uniform(key_of[12], (HEADS,), jnp.float32) ** level_of(key_of[12], (HEADS,), ((0, 2),), -0.2, 0.2), 0.5, 1.5),
        "gate_gain": jnp.clip(1.0 + 0.15 * jax.random.normal(key_of[13], (INNER,), jnp.float32), 0.25, 1.75).astype(jnp.bfloat16),
        "out_proj": noise(key_of[14], (INNER, D), INNER ** -0.5, 0.15625, ((0, 2),)),
        "cotangent": noise(key_of[15], (PACKS, PACK_LEN, D), 1.0, 6.0, ((0, 64),)),
    }


epsilon = 1e-05

@jax.custom_vjp
def low(v):
    return lax.optimization_barrier(v.astype(jnp.bfloat16)).astype(jnp.float32)

@jax.custom_vjp
def low_back(v):
    return v

def low_keep(v):
    return (low(v), None)

def low_pass(kept, grad):
    return (grad,)

def back_keep(v):
    return (v, None)

def back_low(kept, grad):
    return (low(grad),)
low.defvjp(low_keep, low_pass)
low_back.defvjp(back_keep, back_low)

def matmul(left, right):
    return jnp.dot(left, right, precision=lax.Precision.HIGHEST, preferred_element_type=jnp.float32)

def conv_masks(segment, taps):
    length = segment.shape[0]
    padded = jnp.concatenate([jnp.full((taps - 1,), -1, jnp.int32), segment.astype(jnp.int32)])
    return [(padded[taps - 1 - offset:taps - 1 - offset + length] == segment).astype(jnp.float32) for offset in range(taps)]

def causal_conv(values, kernel, shift, masks):
    taps = kernel.shape[0]
    length = values.shape[0]
    padded = jnp.pad(values, ((taps - 1, 0), (0, 0)))
    total = jnp.zeros_like(values) + shift[None, :]
    for offset in range(taps):
        moved = padded[taps - 1 - offset:taps - 1 - offset + length]
        total = total + moved * kernel[taps - 1 - offset][None, :] * masks[offset][:, None]
    return total

def ssd_block(carry, block):
    states, prior_id = carry
    values, step_sizes, log_decay, write_map, read_map, segment = block
    size = segment.shape[0]
    cumlog = jnp.cumsum(log_decay, axis=0)
    places = jnp.arange(size)
    same = (segment[:, None] == segment[None, :]) & (places[:, None] >= places[None, :])
    spread = cumlog[:, None, :] - cumlog[None, :, :]
    decay = jnp.exp(jnp.where(same[:, :, None], spread, 0.0)) * same.astype(jnp.float32)[:, :, None]
    intersection = jnp.dot(read_map, write_map.T, precision=lax.Precision.HIGHEST, preferred_element_type=jnp.float32)
    weights = decay * intersection[:, :, None] * step_sizes[None, :, :]
    inside = jnp.einsum('tsh,shp->thp', weights, values, precision=lax.Precision.HIGHEST)
    entry_scale = (segment == prior_id).astype(jnp.float32)[:, None] * jnp.exp(cumlog)
    across = jnp.einsum('tn,hpn->thp', read_map, states, precision=lax.Precision.HIGHEST) * entry_scale[:, :, None]
    tail_log = cumlog[size - 1]
    last_id = segment[size - 1]
    weight_back = (segment == last_id).astype(jnp.float32)[:, None] * jnp.exp(tail_log[None, :] - cumlog) * step_sizes
    carry_scale = (jnp.exp(tail_log) * (last_id == prior_id).astype(jnp.float32))[:, None, None]
    updates = jnp.einsum('sh,shp,sn->hpn', weight_back, values, write_map, precision=lax.Precision.HIGHEST)
    return ((states * carry_scale + updates, last_id), inside + across)

def state_scan(values, step_sizes, log_decay, write_map, read_map, segment):
    length, head_count, head_dim = values.shape
    block = min(GROUP, length)
    blocks_count = length // block

    def split(member):
        return member.reshape((blocks_count, block) + member.shape[1:])
    start = (jnp.zeros((head_count, head_dim, write_map.shape[1]), jnp.float32), jnp.int32(-1))
    pieces = tuple((split(member) for member in (values, step_sizes, log_decay, write_map, read_map, segment)))
    finished, outputs = lax.scan(jax.checkpoint(ssd_block), start, pieces)
    return outputs.reshape(length, head_count, head_dim)

def mixer(raw_main, state_mix, raw_step, weights, segment):
    conv_kernel, conv_shift, bias_step, rate_log, skip_weight = weights
    length = raw_main.shape[0]
    half_width = raw_main.shape[1] // 2
    gate_in = raw_main[:, :half_width]
    masks = conv_masks(segment, conv_kernel.shape[0])
    main_in = jax.nn.silu(causal_conv(raw_main[:, half_width:], conv_kernel, conv_shift, masks))
    state_width = state_mix.shape[1] // 2
    step_sizes = jax.nn.softplus(raw_step + bias_step[None, :])
    log_decay = -step_sizes * jnp.exp(rate_log)[None, :]
    head_count = bias_step.shape[0]
    values = main_in.reshape(length, head_count, half_width // head_count)
    scanned = state_scan(values, step_sizes, log_decay, state_mix[:, :state_width], state_mix[:, state_width:], segment)
    output = scanned + skip_weight[None, :, None] * values
    return output.reshape(length, half_width) * jax.nn.silu(gate_in)

def layer(params, tokens, segment):
    norm_gain, proj_main, proj_state, proj_step, conv_main, conv_state, bias_main, bias_state, step_bias, log_rate, skip_gain, gate_gain, out_proj = params
    square = lax.optimization_barrier(jnp.mean(tokens * tokens, axis=1, keepdims=True))
    normed = low(tokens * lax.rsqrt(square + epsilon) * norm_gain[None, :])
    main_raw = low_back(matmul(normed, proj_main.reshape(D, 2 * INNER)))
    state_raw = low_back(matmul(normed, proj_state))
    step_raw = low_back(matmul(normed, proj_step))
    masks = conv_masks(segment, CONV)
    state_mix = jax.nn.silu(causal_conv(state_raw, conv_state, bias_state, masks))
    gated = mixer(main_raw, state_mix, step_raw, (conv_main, bias_main, step_bias, log_rate, skip_gain), segment)
    rscale = lax.rsqrt(lax.optimization_barrier(jnp.mean(gated * gated, axis=1, keepdims=True)) + epsilon)
    partial_out = low_back(matmul(low(gated * gate_gain[None, :]), out_proj))
    return tokens + rscale * partial_out

def reference(tokens, segment_ids, norm_gain, proj_main, proj_state, proj_step, conv_main, conv_state, bias_main, bias_state, step_bias, log_rate, skip_gain, gate_gain, out_proj, cotangent):
    params = tuple((member.astype(jnp.float32) for member in (norm_gain, proj_main, proj_state, proj_step, conv_main, conv_state, bias_main, bias_state, step_bias, log_rate, skip_gain, gate_gain, out_proj)))

    def forward(weights, data):

        def one_row(packed):
            return layer(weights, packed[0], packed[1])
        return lax.map(jax.checkpoint(one_row), (data, segment_ids))
    outputs, pull = jax.vjp(forward, params, tokens.astype(jnp.float32))
    grads, grad_data = pull(cotangent.astype(jnp.float32))
    grad_normgain, grad_projmain, grad_projstate, grad_projstep, grad_convmain, grad_convstate, grad_biasmain, grad_biasstate, grad_stepbias, grad_lograte, grad_skipgain, grad_gategain, grad_outproj = grads
    return (outputs.astype(jnp.bfloat16), grad_data.astype(jnp.bfloat16), grad_normgain, grad_projmain, grad_projstate, grad_projstep, grad_convmain, grad_convstate, grad_biasmain, grad_biasstate, grad_stepbias, grad_lograte, grad_skipgain, grad_gategain, grad_outproj)
```

```python
import math

import jax
import jax.numpy as jnp
import numpy as np
from jax import lax
from jax.experimental import pallas as pl
from jax.experimental.pallas import tpu as pltpu
from jax.sharding import PartitionSpec as P

INNER = 1536
TAPS = 4
LANES = 128
HEAD = 64
STATE = 128
CHUNK = 256
HALO = 8
VMEM_BYTES = 56 * 1024 * 1024

epsilon = 1e-05
f32 = jnp.float32
bf16 = jnp.bfloat16

NN = ((1,), (0,))
NT = ((1,), (1,))
TN = ((0,), (0,))


def mm(left, right, dims=NN):
    return lax.dot_general(left, right, (dims, ((), ())), preferred_element_type=f32)


def lane_iota(shape):
    return lax.broadcasted_iota(jnp.int32, shape, 1)


def pack(values, heads):
    values = jnp.where(lane_iota(values.shape) < heads, values, 0.0)
    high = values.astype(bf16).astype(f32)
    rest = values - high
    middle = rest.astype(bf16).astype(f32)
    low = (rest - middle).astype(bf16).astype(f32)
    return (high + pltpu.roll(middle, 16, 1) + pltpu.roll(low, 32, 1)).astype(bf16)


def unpack(values):
    return values + pltpu.roll(values, LANES - 16, 1) + pltpu.roll(values, LANES - 32, 1)


def spread_heads(values, expand, heads):
    return mm(pack(values, heads), expand)


def sum_heads(values, collect):
    high = values.astype(bf16)
    low = (values - high.astype(f32)).astype(bf16)
    return mm(high, collect) + mm(low, collect)


def sigmoid(values):
    return 1.0 / (1.0 + jnp.exp(-values))


def softplus(values):
    return jnp.maximum(values, 0.0) + jnp.log1p(jnp.exp(-jnp.abs(values)))


def half_tile(values, half):
    lane = lane_iota(values.shape)
    keep = lane < HEAD if half == 0 else lane >= HEAD
    return jnp.where(keep, values, jnp.zeros_like(values))


def norm_scale(data):
    return lax.rsqrt(jnp.mean(data * data, axis=1, keepdims=True) + epsilon)


def scan_sizes(raw_step, step_bias, neg_rate, aux, heads, length):
    step = softplus(raw_step + step_bias)
    logdecay = step * neg_rate
    places = lax.broadcasted_iota(jnp.int32, (length, length), 0)
    others = lax.broadcasted_iota(jnp.int32, (length, length), 1)
    lower = (places >= others).astype(bf16)
    cumlog = unpack(mm(lower, pack(logdecay, heads)))
    entry = aux[:, 7:8] * jnp.exp(cumlog)
    back = aux[:, 8:9] * jnp.exp(cumlog[length - 1 : length] - cumlog)
    return step, logdecay, cumlog, entry, back


def forward_kernel(heads, tokens, aux, seg_row, cotangent, norm_gain, wall, taps, tap_bias,
                   step_bias, neg_rate, skip, gate_gain, out_proj, expand,
                   normed_out, raw_out, pre_out, y_out, scaled_out, partial_out, stats_out,
                   state_out, state, halo):
    length = tokens.shape[0]
    width = gate_gain.shape[1]
    mixed_width = width + 2 * STATE

    @pl.when(pl.program_id(0) == 0)
    def _():
        state[...] = jnp.zeros_like(state)
        halo[0:HALO, :] = jnp.zeros((HALO, mixed_width), f32)

    data = tokens[...].astype(f32)
    normed = (data * norm_scale(data) * norm_gain[...]).astype(bf16)
    normed_out[...] = normed
    raw = mm(normed, wall[...])
    raw_out[...] = raw
    mixer = raw[:, width : width + mixed_width]
    halo[HALO : HALO + length, :] = mixer
    masks = aux[...]
    pre = tap_bias[...] + mixer * taps[TAPS - 1 : TAPS, :]
    for offset in range(1, TAPS):
        moved = halo[HALO - offset : HALO - offset + length, :]
        pre += moved * taps[TAPS - 1 - offset : TAPS - offset, :] * masks[:, offset : offset + 1]
    halo[0:HALO, :] = halo[length : length + HALO, :]
    pre_out[...] = pre
    act = pre * sigmoid(pre)
    values = act[:, :width]
    write = act[:, width : width + STATE].astype(bf16)
    read = act[:, width + STATE :].astype(bf16)
    step, _, cumlog, entry, back = scan_sizes(
        raw[:, width + mixed_width :], step_bias[...], neg_rate[...], masks, heads, length
    )
    entry_wide = spread_heads(entry, expand[...], heads)
    back_wide = spread_heads(back, expand[...], heads)
    stepped = values * spread_heads(step, expand[...], heads)
    before = state[...]
    state_out[0] = before
    across = mm(read, before.astype(bf16)) * entry_wide
    state[...] = before * entry_wide[length - 1 : length, :] + mm(
        write, (stepped * back_wide).astype(bf16), TN
    )
    similar = mm(read, write, NT)
    places = lax.broadcasted_iota(jnp.int32, (length, length), 0)
    others = lax.broadcasted_iota(jnp.int32, (length, length), 1)
    open_pair = (masks[:, 0:1] == seg_row[...]) & (places >= others)
    shut = jnp.where(open_pair, 0.0, -1e30)
    cum_rows = jnp.transpose(cumlog)
    stepped_low = stepped.astype(bf16)
    tiles = []
    for pair in range(heads // 2):
        tile = stepped_low[:, pair * LANES : (pair + 1) * LANES]
        total = None
        for half in range(2):
            head = 2 * pair + half
            decay = jnp.exp(cumlog[:, head : head + 1] - cum_rows[head : head + 1, :] + shut)
            term = mm((decay * similar).astype(bf16), half_tile(tile, half))
            total = term if total is None else total + term
        tiles.append(total)
    y = jnp.concatenate(tiles, axis=1) + across + skip[...] * values
    y_out[...] = y
    gate = raw[:, :width]
    gated = y * (gate * sigmoid(gate))
    squares = jnp.sum(gated * gated, axis=1, keepdims=True)
    scaled = (gated * gate_gain[...]).astype(bf16)
    scaled_out[...] = scaled
    partial = mm(scaled, out_proj[...])
    partial_out[...] = partial
    along = jnp.sum(cotangent[...].astype(f32) * partial, axis=1, keepdims=True)
    lane = lane_iota((length, LANES))
    stats = jnp.where(lane == 0, squares, jnp.where(lane == 1, along, 0.0))
    stats_out[...] = jnp.transpose(stats)[0:8, :]


def backward_kernel(heads, tokens, aux, seg_row, cotangent, norm_gain, wall, taps,
                    step_bias, neg_rate, skip, gate_gain, out_proj, expand, collect,
                    raw_in, pre_in, y_in, scales, state_in,
                    back_out, joined_out, grad_norm, grad_taps,
                    grad_heads, grad_gate, state_grad, halo):
    length = tokens.shape[0]
    width = gate_gain.shape[1]
    mixed_width = width + 2 * STATE

    @pl.when(pl.program_id(0) == 0)
    def _():
        state_grad[...] = jnp.zeros_like(state_grad)
        halo[length : length + HALO, :] = jnp.zeros((HALO, mixed_width), f32)
        for member in (grad_norm, grad_taps, grad_heads, grad_gate):
            member[...] = jnp.zeros_like(member)

    masks = aux[...]
    columns = jnp.transpose(jnp.concatenate([scales[...], jnp.zeros((LANES - 8, length), f32)], 0))
    rscale = columns[:, 0:1]
    ratio = columns[:, 1:2]
    grad_part = (rscale * cotangent[...].astype(f32)).astype(bf16)
    grad_scaled = mm(grad_part, out_proj[...], NT)
    gate = raw_in[:, :width]
    gate_sig = sigmoid(gate)
    gate_silu = gate * gate_sig
    y = y_in[...]
    gated = y * gate_silu
    grad_gate[0:1, :] += jnp.sum(grad_scaled * gated, axis=0, keepdims=True)
    grad_gated = grad_scaled * gate_gain[...] - ratio * gated * (1.0 / INNER)
    grad_y = grad_gated * gate_silu
    grad_z = grad_gated * y * (gate_sig * (1.0 + gate * (1.0 - gate_sig)))

    pre = pre_in[...]
    pre_sig = sigmoid(pre)
    act = pre * pre_sig
    values = act[:, :width]
    write = act[:, width : width + STATE].astype(bf16)
    read = act[:, width + STATE :].astype(bf16)
    raw_step = raw_in[:, width + mixed_width :]
    step, logdecay, cumlog, entry, back = scan_sizes(
        raw_step, step_bias[...], neg_rate[...], masks, heads, length
    )
    entry_wide = spread_heads(entry, expand[...], heads)
    back_wide = spread_heads(back, expand[...], heads)
    step_wide = spread_heads(step, expand[...], heads)
    stepped = values * step_wide
    before = state_in[0]
    before_low = before.astype(bf16)
    after_grad = state_grad[...]
    after_low = after_grad.astype(bf16)
    grad_entry = grad_y * entry_wide
    grad_entry_low = grad_entry.astype(bf16)
    grad_y_low = grad_y.astype(bf16)
    stepped_low = stepped.astype(bf16)
    stepped_back = stepped * back_wide
    from_entry = sum_heads(grad_entry * mm(read, before_low), collect[...])
    grad_read = mm(grad_entry_low, before_low, NT)
    carried = mm(write, after_low)
    from_back = sum_heads(stepped_back * carried, collect[...])
    grad_write = mm(stepped_back.astype(bf16), after_low, NT)
    overlap = jnp.sum(before * after_grad, axis=0, keepdims=True) * entry_wide[length - 1 : length, :]
    overlap = sum_heads(jnp.broadcast_to(overlap, (8, width)), collect[...])[0:1, :]
    state_grad[...] = after_grad * entry_wide[length - 1 : length, :] + mm(read, grad_entry_low, TN)

    similar = mm(write, read, NT)
    places = lax.broadcasted_iota(jnp.int32, (length, length), 0)
    others = lax.broadcasted_iota(jnp.int32, (length, length), 1)
    open_pair = (masks[:, 0:1] == seg_row[...]) & (places <= others)
    shut = jnp.where(open_pair, 0.0, -1e30)
    cum_rows = jnp.transpose(cumlog)
    lane = lane_iota((length, LANES))
    grad_similar = jnp.zeros((length, length), f32)
    from_source = jnp.zeros((length, LANES), f32)
    target_rows = []
    tiles = []
    for pair in range(heads // 2):
        span = slice(pair * LANES, (pair + 1) * LANES)
        total = None
        for half in range(2):
            head = 2 * pair + half
            decay = jnp.exp(cum_rows[head : head + 1, :] - cumlog[:, head : head + 1] + shut)
            weights = decay * similar
            grad_half = half_tile(grad_y_low[:, span], half)
            term = mm(weights.astype(bf16), grad_half)
            total = term if total is None else total + term
            grad_decayed = mm(stepped_low[:, span], grad_half, NT)
            grad_similar += grad_decayed * decay
            product = grad_decayed * weights
            from_source = jnp.where(lane == head, jnp.sum(product, axis=1, keepdims=True), from_source)
            target_rows.append(jnp.sum(product, axis=0, keepdims=True))
        tiles.append(total)
    target_rows.append(jnp.zeros((LANES - heads, length), f32))
    from_target = jnp.transpose(jnp.concatenate(target_rows, axis=0))
    grad_similar_low = grad_similar.astype(bf16)
    grad_write += mm(grad_similar_low, read)
    grad_read += mm(grad_similar_low, write, TN)
    grad_stepped = jnp.concatenate(tiles, axis=1) + back_wide * carried

    grad_cumlog = from_entry - from_back + from_target - from_source
    upper = (places <= others).astype(bf16)
    grad_log = unpack(mm(upper, pack(grad_cumlog, heads)))
    grad_log += jnp.sum(from_back, axis=0, keepdims=True) + overlap
    grad_log = jnp.where(lane < heads, grad_log, 0.0)
    grad_step = sum_heads(grad_stepped * values, collect[...]) + neg_rate[...] * grad_log
    grad_rawstep = grad_step * sigmoid(raw_step + step_bias[...])
    grad_heads[0:1, :] += jnp.sum(grad_rawstep, axis=0, keepdims=True)
    grad_heads[1:2, :] += jnp.sum(grad_log * logdecay, axis=0, keepdims=True)
    skipped = jnp.sum(grad_y * values, axis=0, keepdims=True)
    grad_heads[2:3, :] += sum_heads(jnp.broadcast_to(skipped, (8, width)), collect[...])[0:1, :]
    grad_values = grad_stepped * step_wide + skip[...] * grad_y
    grad_pre = jnp.concatenate([grad_values, grad_write, grad_read], axis=1) * (
        pre_sig * (1.0 + pre * (1.0 - pre_sig))
    )
    halo[0:length, :] = grad_pre
    mixer = raw_in[:, width : width + mixed_width]
    grad_mixer = grad_pre * taps[TAPS - 1 : TAPS, :]
    grad_taps[TAPS - 1 : TAPS, :] += jnp.sum(grad_pre * mixer, axis=0, keepdims=True)
    grad_taps[TAPS : TAPS + 1, :] += jnp.sum(grad_pre, axis=0, keepdims=True)
    for offset in range(1, TAPS):
        place = TAPS - 1 - offset
        moved = halo[offset : offset + length, :] * masks[:, 3 + offset : 4 + offset]
        grad_mixer += moved * taps[place : place + 1, :]
        grad_taps[place : place + 1, :] += jnp.sum(moved * mixer, axis=0, keepdims=True)
    halo[length : length + HALO, :] = halo[0:HALO, :]
    joined = jnp.concatenate(
        [grad_z.astype(bf16), grad_mixer.astype(bf16), grad_rawstep.astype(bf16)], axis=1
    )
    grad_input = mm(joined, wall[...], NT)
    joined_out[...] = joined
    data = tokens[...].astype(f32)
    scale = norm_scale(data)
    grad_norm[0:1, :] += jnp.sum(grad_input * data * scale, axis=0, keepdims=True)
    gained = grad_input * norm_gain[...]
    back_out[...] = gained * scale - data * (
        scale * scale * scale * jnp.mean(gained * data, axis=1, keepdims=True)
    )


def side_columns(segment, chunk):
    length = segment.shape[0]
    columns = [segment]
    before = jnp.concatenate([jnp.full((TAPS - 1,), -1, jnp.int32), segment])
    after = jnp.concatenate([segment, jnp.full((TAPS - 1,), -1, jnp.int32)])
    for offset in range(1, TAPS):
        columns.append(before[TAPS - 1 - offset : TAPS - 1 - offset + length] == segment)
    for offset in range(1, TAPS):
        columns.append(after[offset : offset + length] == segment)
    blocks = segment.reshape(length // chunk, chunk)
    last = blocks[:, chunk - 1]
    prior = jnp.concatenate([jnp.full((1,), -1, jnp.int32), last[:-1]])
    columns.append((blocks == prior[:, None]).reshape(length))
    columns.append((blocks == last[:, None]).reshape(length))
    stacked = jnp.stack([member.astype(f32) for member in columns], axis=1)
    return jnp.pad(stacked, ((0, 0), (0, LANES - len(columns))))


def pad_heads(values):
    return jnp.pad(values, (0, LANES - values.shape[0])).reshape(1, LANES)


def local(
    tokens,
    segment_ids,
    norm_gain,
    proj_main,
    proj_state,
    proj_step,
    conv_main,
    conv_state,
    bias_main,
    bias_state,
    step_bias,
    log_rate,
    skip_gain,
    gate_gain,
    out_proj,
    cotangent,
):
    packs, length, model = tokens.shape
    width = proj_main.shape[2]
    heads = step_bias.shape[0]
    state_cols = proj_state.shape[1]
    mixed_width = width + state_cols
    wall_cols = width + mixed_width + LANES
    chunk = min(CHUNK, length)
    count = length // chunk
    data = tokens.reshape(length, model)
    cot = cotangent.reshape(length, model)
    wall = jnp.concatenate(
        [
            proj_main[:, 0],
            proj_main[:, 1],
            proj_state,
            jnp.pad(proj_step, ((0, 0), (0, LANES - heads))),
        ],
        axis=1,
    )
    taps = jnp.concatenate([conv_main, conv_state], axis=1)
    tap_bias = jnp.concatenate([bias_main, bias_state]).reshape(1, mixed_width)
    step_row = pad_heads(step_bias)
    neg_rate = pad_heads(-jnp.exp(log_rate))
    skip = jnp.repeat(skip_gain, HEAD).reshape(1, width)
    gain_row = norm_gain.astype(f32).reshape(1, model)
    gate_row = gate_gain.astype(f32).reshape(1, width)
    aux = side_columns(segment_ids[0], chunk)
    seg_row = segment_ids.astype(f32)
    places = np.arange(LANES)[:, None]
    owner = np.arange(width)[None, :] // HEAD
    expand = jnp.asarray((places % 16 == owner) & (places < 48), bf16)
    collect = jnp.asarray((places == owner).T, bf16)

    def whole(shape):
        return pl.BlockSpec(shape, lambda i: (0,) * len(shape))

    def specs(order):
        def rows(cols):
            return pl.BlockSpec((chunk, cols), lambda i: (order(i), 0))

        def wide(count_rows):
            return pl.BlockSpec((count_rows, chunk), lambda i: (0, order(i)))

        state = pl.BlockSpec((1, STATE, width), lambda i: (order(i), 0, 0))
        return rows, wide, state

    params = pltpu.CompilerParams(
        dimension_semantics=("arbitrary",), vmem_limit_bytes=VMEM_BYTES
    )
    rows, wide, state_spec = specs(lambda i: i)
    normed, raw, pre, y, scaled, partial, stats, states = pl.pallas_call(
        lambda *refs: forward_kernel(heads, *refs),
        grid=(count,),
        in_specs=[
            rows(model), rows(LANES), wide(1), rows(model), whole((1, model)),
            whole((model, wall_cols)), whole((TAPS, mixed_width)), whole((1, mixed_width)),
            whole((1, LANES)), whole((1, LANES)), whole((1, width)), whole((1, width)),
            whole((width, model)), whole((LANES, width)),
        ],
        out_specs=[
            rows(model), rows(wall_cols), rows(mixed_width), rows(width), rows(width),
            rows(model), wide(8), state_spec,
        ],
        out_shape=[
            jax.ShapeDtypeStruct((length, model), bf16),
            jax.ShapeDtypeStruct((length, wall_cols), f32),
            jax.ShapeDtypeStruct((length, mixed_width), f32),
            jax.ShapeDtypeStruct((length, width), f32),
            jax.ShapeDtypeStruct((length, width), bf16),
            jax.ShapeDtypeStruct((length, model), f32),
            jax.ShapeDtypeStruct((8, length), f32),
            jax.ShapeDtypeStruct((count, STATE, width), f32),
        ],
        scratch_shapes=[
            pltpu.VMEM((STATE, width), f32),
            pltpu.VMEM((chunk + HALO, mixed_width), f32),
        ],
        compiler_params=params,
        cost_estimate=pl.CostEstimate(
            flops=15_000_000_000, bytes_accessed=30_000_000, transcendentals=5_000_000
        ),
    )(data, aux, seg_row, cot, gain_row, wall, taps, tap_bias, step_row, neg_rate, skip,
      gate_row, out_proj, expand)

    swap = [(0, 1), (1, 0)]
    totals = stats[:2] + lax.ppermute(stats[:2], "tensor", swap)
    rscale = lax.rsqrt(totals[0] / INNER + epsilon)
    ratio = totals[1] * rscale * rscale * rscale
    scales = jnp.pad(jnp.stack([rscale, ratio]), ((0, 6), (0, 0)))
    other = lax.ppermute(partial, "tensor", swap)

    cot_wide = cot.astype(f32)
    grad_part = (rscale[:, None] * cot_wide).astype(bf16)
    grad_outproj = scatter_sum(grad_part, scaled, "xyz")

    rows, wide, state_spec = specs(lambda i: count - 1 - i)
    back, joined, grad_norm, grad_taps, grad_heads, grad_gate = pl.pallas_call(
        lambda *refs: backward_kernel(heads, *refs),
        grid=(count,),
        in_specs=[
            rows(model), rows(LANES), wide(1), rows(model), whole((1, model)),
            whole((model, wall_cols)), whole((TAPS, mixed_width)),
            whole((1, LANES)), whole((1, LANES)), whole((1, width)), whole((1, width)),
            whole((width, model)), whole((LANES, width)), whole((width, LANES)),
            rows(wall_cols), rows(mixed_width), rows(width), wide(8), state_spec,
        ],
        out_specs=[
            rows(model), rows(wall_cols), whole((8, model)),
            whole((8, mixed_width)), whole((8, LANES)), whole((8, width)),
        ],
        out_shape=[
            jax.ShapeDtypeStruct((length, model), f32),
            jax.ShapeDtypeStruct((length, wall_cols), bf16),
            jax.ShapeDtypeStruct((8, model), f32),
            jax.ShapeDtypeStruct((8, mixed_width), f32),
            jax.ShapeDtypeStruct((8, LANES), f32),
            jax.ShapeDtypeStruct((8, width), f32),
        ],
        scratch_shapes=[
            pltpu.VMEM((STATE, width), f32),
            pltpu.VMEM((chunk + HALO, mixed_width), f32),
        ],
        compiler_params=params,
        cost_estimate=pl.CostEstimate(
            flops=30_000_000_000, bytes_accessed=60_000_000, transcendentals=6_000_000
        ),
    )(data, aux, seg_row, cot, gain_row, wall, taps, step_row, neg_rate, skip, gate_row,
      out_proj, expand, collect, raw, pre, y, scales, states)

    mixed = (data.astype(f32) + rscale[:, None] * (partial + other)).astype(bf16)
    back_sum = back + lax.ppermute(back, "tensor", swap)
    grad_tokens = (cot_wide + back_sum).astype(bf16)

    wall_pad = -wall_cols % (2 * LANES)
    reduced = scatter_sum(normed, jnp.pad(joined, ((0, 0), (0, wall_pad))), "yxz")
    grad_state = reduced[:, 2 * width : width + mixed_width]
    grad_state = grad_state + lax.ppermute(grad_state, "tensor", swap)

    own = [grad_taps[:, :width], grad_heads, grad_gate]
    shared = jnp.concatenate([grad_norm, grad_taps[:, width:]], axis=1)
    shared = shared + lax.ppermute(shared, "tensor", swap)
    summed = share_sum(jnp.concatenate([*own, shared], axis=1)[:5])
    cuts = np.cumsum([width, LANES, width, model])
    own_taps, own_heads, own_gate, norm_part, shared_taps = jnp.split(summed, cuts, axis=1)
    return (
        mixed.reshape(tokens.shape),
        grad_tokens.reshape(tokens.shape),
        norm_part[0],
        reduced[:, : 2 * width].reshape(-1, 2, width),
        grad_state,
        reduced[:, width + mixed_width : width + mixed_width + heads],
        own_taps[:TAPS],
        shared_taps[:TAPS],
        own_taps[TAPS],
        shared_taps[TAPS],
        own_heads[0, :heads],
        own_heads[1, :heads],
        own_heads[2, :heads],
        own_gate[0],
        grad_outproj.T,
    )


RINGS = (("y", 4), ("z", 2), ("x", 4), ("core", 2))


def ring_place(index, ring):
    for name, size in reversed(RINGS):
        if name == ring:
            return index % size
        index = index // size


def ring_shift(values, ring, step):
    pairs = []
    for source in range(math.prod(size for _, size in RINGS)):
        stride = 1
        for name, size in reversed(RINGS):
            if name == ring:
                place = source // stride % size
                pairs.append((source, source + ((place + step) % size - place) * stride))
            stride *= size
    return lax.ppermute(values, "dp", pairs)


def scatter_sum(left, right, order):
    index = lax.axis_index("dp")
    core = ring_place(index, "core")
    half = right.shape[1] // 2

    def product(which):
        return mm(left, lax.dynamic_slice_in_dim(right, which * half, half, axis=1), TN)

    away = ring_shift(product(1 - core), "core", 1)
    total = product(core) + away
    sizes = dict(RINGS)
    rings = [name for name, _ in RINGS if name != "core"]
    rows = total.shape[0] // math.prod(sizes[name] for name in rings)
    total = total.reshape([sizes[name] for name in rings] + [rows, half])
    for ring in order:
        axis, size = rings.index(ring), sizes[ring]
        place = ring_place(index, ring)
        parts = [
            lax.dynamic_index_in_dim(total, (place + step) % size, axis, keepdims=False)
            for step in range(size)
        ]
        total = parts[0]
        for step in range(1, size):
            total = total + ring_shift(parts[step], ring, step)
        rings.remove(ring)
    share = rows // 2
    mine = lax.dynamic_slice_in_dim(total, core * share, share, axis=0)
    other = lax.dynamic_slice_in_dim(total, (1 - core) * share, share, axis=0)
    other = ring_shift(other, "core", 1)
    return jnp.where(
        core == 0,
        jnp.concatenate([mine, other], axis=1),
        jnp.concatenate([other, mine], axis=1),
    )


def share_sum(values):
    for ring, size in reversed(RINGS):
        moved = [ring_shift(values, ring, step) for step in range(1, size)]
        for member in moved:
            values = values + member
    return values


def solution(mesh):
    placed = (
        P("dp", None, None),
        P("dp", None),
        P(),
        P(None, None, "tensor"),
        P(),
        P(None, "tensor"),
        P(None, "tensor"),
        P(),
        P("tensor"),
        P(),
        P("tensor"),
        P("tensor"),
        P("tensor"),
        P("tensor"),
        P("tensor", None),
        P("dp", None, None),
    )
    return jax.shard_map(
        local,
        mesh=mesh,
        in_specs=placed,
        out_specs=(
            P("dp", None, None),
            P("dp", None, None),
            P(),
            P("dp", None, "tensor"),
            P("dp", None),
            P("dp", "tensor"),
            P(None, "tensor"),
            P(),
            P("tensor"),
            P(),
            P("tensor"),
            P("tensor"),
            P("tensor"),
            P("tensor"),
            P("tensor", "dp"),
        ),
        check_vma=False,
    )
```

```python
import math

import jax
import jax.numpy as jnp
import numpy as np
from jax import lax
from jax.experimental import pallas as pl
from jax.experimental.pallas import tpu as pltpu
from jax.sharding import PartitionSpec as P

INNER = 1536
TAPS = 4
LANES = 128
HEAD = 64
STATE = 128
CHUNK = 256
HALO = 8
VMEM_BYTES = 56 * 1024 * 1024

epsilon = 1e-05
f32 = jnp.float32
bf16 = jnp.bfloat16

NN = ((1,), (0,))
NT = ((1,), (1,))
TN = ((0,), (0,))


def mm(left, right, dims=NN):
    return lax.dot_general(left, right, (dims, ((), ())), preferred_element_type=f32)


def lane_iota(shape):
    return lax.broadcasted_iota(jnp.int32, shape, 1)


def pack(values, heads):
    values = jnp.where(lane_iota(values.shape) < heads, values, 0.0)
    high = values.astype(bf16).astype(f32)
    rest = values - high
    middle = rest.astype(bf16).astype(f32)
    low = (rest - middle).astype(bf16).astype(f32)
    return (high + pltpu.roll(middle, 16, 1) + pltpu.roll(low, 32, 1)).astype(bf16)


def unpack(values):
    return values + pltpu.roll(values, LANES - 16, 1) + pltpu.roll(values, LANES - 32, 1)


def spread_heads(values, expand, heads):
    return mm(pack(values, heads), expand)


def sum_heads(values, collect):
    high = values.astype(bf16)
    low = (values - high.astype(f32)).astype(bf16)
    return mm(high, collect) + mm(low, collect)


def sigmoid(values):
    return 1.0 / (1.0 + jnp.exp(-values))


def softplus(values):
    return jnp.maximum(values, 0.0) + jnp.log1p(jnp.exp(-jnp.abs(values)))


def half_tile(values, half):
    lane = lane_iota(values.shape)
    keep = lane < HEAD if half == 0 else lane >= HEAD
    return jnp.where(keep, values, jnp.zeros_like(values))


def norm_scale(data):
    return lax.rsqrt(jnp.mean(data * data, axis=1, keepdims=True) + epsilon)


def scan_sizes(raw_step, step_bias, neg_rate, from_prior, to_last, heads, length):
    step = softplus(raw_step + step_bias)
    logdecay = step * neg_rate
    places = lax.broadcasted_iota(jnp.int32, (length, length), 0)
    others = lax.broadcasted_iota(jnp.int32, (length, length), 1)
    lower = (places >= others).astype(bf16)
    cumlog = unpack(mm(lower, pack(logdecay, heads)))
    entry = from_prior * jnp.exp(cumlog)
    back = to_last * jnp.exp(cumlog[length - 1 : length] - cumlog)
    return step, logdecay, cumlog, entry, back


def segment_columns(seg_row, seg_scalar, rows, place, length):
    total = seg_row.shape[1]
    full = jnp.broadcast_to(seg_row[...].astype(f32), (8, total))
    lane = lane_iota((8, total))
    sub = lax.broadcasted_iota(jnp.int32, (8, total), 0)
    table = full
    for offset in range(1, TAPS):
        before = (pltpu.roll(full, offset, 1) == full) & (lane >= offset)
        after = (pltpu.roll(full, total - offset, 1) == full) & (lane < total - offset)
        table = jnp.where(sub == offset, jnp.where(before, 1.0, 0.0), table)
        table = jnp.where(sub == TAPS - 1 + offset, jnp.where(after, 1.0, 0.0), table)
    rows[...] = table
    start = pl.multiple_of(place * length, length)
    here = rows[:, pl.ds(start, length)]
    columns = jnp.transpose(
        jnp.concatenate([here, jnp.zeros((LANES - 8, length), f32)], axis=0)
    )
    prior = jnp.where(place == 0, -1, seg_scalar[0, jnp.maximum(start - 1, 0)]).astype(f32)
    last = seg_scalar[0, start + length - 1].astype(f32)
    own = columns[:, 0:1]
    from_prior = jnp.where(own == prior, 1.0, 0.0)
    to_last = jnp.where(own == last, 1.0, 0.0)
    return columns, here[0:1, :], from_prior, to_last


def forward_kernel(heads, first, kept, spans, *refs):
    (tokens, seg_row, seg_scalar, cotangent, rows, wmain, wstate, wstep, taps, tap_bias,
     out_proj, expand) = refs[:12]
    refs = refs[12:]
    if first:
        state_in, halo_in = refs[:2]
        refs = refs[2 + kept :]
    (normed_out, raw_out, pre_out, y_out, scaled_out, stats_out, state_out,
     state, halo_out) = refs[:9]
    partial_outs = refs[9:-2]
    halo, seg_rows = refs[-2:]
    norm_gain, gate_gain, skip, step_bias, neg_rate = (
        rows[k : k + 1, :] for k in range(5)
    )
    step_bias, neg_rate = step_bias[:, :LANES], neg_rate[:, :LANES]
    length = tokens.shape[0]
    width = wmain.shape[1] // 2
    mixed_width = width + 2 * STATE
    step_index = pl.program_id(0)

    @pl.when(step_index == 0)
    def _():
        if first:
            state[...] = state_in[...]
            halo[0:HALO, :] = halo_in[...]
        else:
            state[...] = jnp.zeros_like(state)
            halo[0:HALO, :] = jnp.zeros((HALO, mixed_width), f32)

    masks, seg_here, from_prior, to_last = segment_columns(
        seg_row, seg_scalar, seg_rows, step_index + first, length
    )
    data = tokens[...].astype(f32)
    normed = (data * norm_scale(data) * norm_gain).astype(bf16)
    normed_out[...] = normed
    raw_main = mm(normed, wmain[...])
    mixer = jnp.concatenate([raw_main[:, width:], mm(normed, wstate[...])], axis=1)
    raw_step = mm(normed, wstep[...])
    raw_out[:, :width] = raw_main[:, :width]
    raw_out[:, width : width + mixed_width] = mixer
    raw_out[:, width + mixed_width :] = raw_step
    halo[HALO : HALO + length, :] = mixer
    pre = tap_bias[...] + mixer * taps[TAPS - 1 : TAPS, :]
    for offset in range(1, TAPS):
        moved = halo[HALO - offset : HALO - offset + length, :]
        pre += moved * taps[TAPS - 1 - offset : TAPS - offset, :] * masks[:, offset : offset + 1]
    halo[0:HALO, :] = halo[length : length + HALO, :]
    halo_out[...] = halo[0:HALO, :]
    pre_out[...] = pre
    act = pre * sigmoid(pre)
    values = act[:, :width]
    write = act[:, width : width + STATE].astype(bf16)
    read = act[:, width + STATE :].astype(bf16)
    step, _, cumlog, entry, back = scan_sizes(
        raw_step, step_bias, neg_rate, from_prior, to_last, heads, length
    )
    entry_wide = spread_heads(entry, expand[...], heads)
    back_wide = spread_heads(back, expand[...], heads)
    stepped = values * spread_heads(step, expand[...], heads)
    before = state[...]
    state_out[0] = before
    across = mm(read, before.astype(bf16)) * entry_wide
    state[...] = before * entry_wide[length - 1 : length, :] + mm(
        write, (stepped * back_wide).astype(bf16), TN
    )
    similar = mm(read, write, NT)
    places = lax.broadcasted_iota(jnp.int32, (length, length), 0)
    others = lax.broadcasted_iota(jnp.int32, (length, length), 1)
    open_pair = (masks[:, 0:1] == seg_here) & (places >= others)
    shut = jnp.where(open_pair, 0.0, -1e30)
    cum_rows = jnp.transpose(cumlog)
    stepped_low = stepped.astype(bf16)
    tiles = []
    for pair in range(heads // 2):
        tile = stepped_low[:, pair * LANES : (pair + 1) * LANES]
        total = None
        for half in range(2):
            head = 2 * pair + half
            decay = jnp.exp(cumlog[:, head : head + 1] - cum_rows[head : head + 1, :] + shut)
            term = mm((decay * similar).astype(bf16), half_tile(tile, half))
            total = term if total is None else total + term
        tiles.append(total)
    y = jnp.concatenate(tiles, axis=1) + across + skip * values
    y_out[...] = y
    gate = raw_main[:, :width]
    gated = y * (gate * sigmoid(gate))
    squares = jnp.sum(gated * gated, axis=1, keepdims=True)
    scaled = (gated * gate_gain).astype(bf16)
    scaled_out[...] = scaled
    partial = mm(scaled, out_proj[...])
    for order in range(spans[-1] // length):

        @pl.when(step_index == order)
        def _(begin=order * length):
            low = 0
            for high, partial_out in zip(spans, partial_outs):
                left, right = max(low, begin), min(high, begin + length)
                if left < right:
                    partial_out[left - low : right - low, :] = partial[left - begin : right - begin]
                low = high

    along = jnp.sum(cotangent[...].astype(f32) * partial, axis=1, keepdims=True)
    lane = lane_iota((length, LANES))
    stats = jnp.where(lane == 0, squares, jnp.where(lane == 1, along, 0.0))
    stats_out[...] = jnp.transpose(stats)[0:8, :]


def backward_kernel(heads, place, resumed, marks, *refs):
    (tokens, seg_row, seg_scalar, cotangent, rows, wmain_far, wstate, wstep, taps,
     out_proj, expand, collect, raw_in, pre_in, y_in, scales, state_in) = refs[:17]
    refs = refs[17:]
    if resumed:
        state_grad_in, halo_in, small_in = refs[:3]
        refs = refs[4:]
    refs = refs[marks:]
    (joined_out, back_out, state_grad, halo_out, small,
     halo, seg_rows, wmain, arrived) = refs
    norm_gain, gate_gain, skip, step_bias, neg_rate = (
        rows[k : k + 1, :] for k in range(5)
    )
    step_bias, neg_rate = step_bias[:, :LANES], neg_rate[:, :LANES]
    length = tokens.shape[0]
    width = wmain.shape[1] // 2
    model = tokens.shape[1]
    mixed_width = width + 2 * STATE
    fetch = pltpu.make_async_copy(wmain_far, wmain, arrived)
    step_index = pl.program_id(0)

    @pl.when(step_index == 0)
    def _():
        fetch.start()
        if resumed:
            state_grad[...] = state_grad_in[...]
            halo[length : length + HALO, :] = halo_in[...]
            small[...] = small_in[...]
        else:
            halo[length : length + HALO, :] = jnp.zeros((HALO, mixed_width), f32)
            for member in (state_grad, small):
                member[...] = jnp.zeros_like(member)

    masks, seg_here, from_prior, to_last = segment_columns(
        seg_row, seg_scalar, seg_rows, place - step_index, length
    )
    zeros = jnp.zeros((LANES - 8, length), f32)
    columns = jnp.transpose(jnp.concatenate([scales[...], zeros], 0))
    rscale = columns[:, 0:1]
    ratio = columns[:, 1:2]
    grad_part = (rscale * cotangent[...].astype(f32)).astype(bf16)
    grad_scaled = mm(grad_part, out_proj[...], NT)
    gate = raw_in[:, :width]
    gate_sig = sigmoid(gate)
    gate_silu = gate * gate_sig
    y = y_in[...]
    gated = y * gate_silu
    small[6:7, :width] += jnp.sum(grad_scaled * gated, axis=0, keepdims=True)
    grad_gated = grad_scaled * gate_gain - ratio * gated * (1.0 / INNER)
    grad_y = grad_gated * gate_silu
    grad_z = grad_gated * y * (gate_sig * (1.0 + gate * (1.0 - gate_sig)))

    pre = pre_in[...]
    pre_sig = sigmoid(pre)
    act = pre * pre_sig
    values = act[:, :width]
    write = act[:, width : width + STATE].astype(bf16)
    read = act[:, width + STATE :].astype(bf16)
    raw_step = raw_in[:, width + mixed_width :]
    step, logdecay, cumlog, entry, back = scan_sizes(
        raw_step, step_bias, neg_rate, from_prior, to_last, heads, length
    )
    entry_wide = spread_heads(entry, expand[...], heads)
    back_wide = spread_heads(back, expand[...], heads)
    step_wide = spread_heads(step, expand[...], heads)
    stepped = values * step_wide
    before = state_in[0]
    before_low = before.astype(bf16)
    after_grad = state_grad[...]
    after_low = after_grad.astype(bf16)
    grad_entry = grad_y * entry_wide
    grad_entry_low = grad_entry.astype(bf16)
    grad_y_low = grad_y.astype(bf16)
    stepped_low = stepped.astype(bf16)
    stepped_back = stepped * back_wide
    from_entry = sum_heads(grad_entry * mm(read, before_low), collect[...])
    grad_read = mm(grad_entry_low, before_low, NT)
    carried = mm(write, after_low)
    from_back = sum_heads(stepped_back * carried, collect[...])
    grad_write = mm(stepped_back.astype(bf16), after_low, NT)
    overlap = jnp.sum(before * after_grad, axis=0, keepdims=True) * entry_wide[length - 1 : length, :]
    overlap = sum_heads(jnp.broadcast_to(overlap, (8, width)), collect[...])[0:1, :]
    state_grad[...] = after_grad * entry_wide[length - 1 : length, :] + mm(read, grad_entry_low, TN)

    similar = mm(write, read, NT)
    places = lax.broadcasted_iota(jnp.int32, (length, length), 0)
    others = lax.broadcasted_iota(jnp.int32, (length, length), 1)
    open_pair = (masks[:, 0:1] == seg_here) & (places <= others)
    shut = jnp.where(open_pair, 0.0, -1e30)
    cum_rows = jnp.transpose(cumlog)
    lane = lane_iota((length, LANES))
    grad_similar = jnp.zeros((length, length), f32)
    from_source = jnp.zeros((length, LANES), f32)
    target_rows = []
    tiles = []
    for pair in range(heads // 2):
        span = slice(pair * LANES, (pair + 1) * LANES)
        total = None
        for half in range(2):
            head = 2 * pair + half
            decay = jnp.exp(cum_rows[head : head + 1, :] - cumlog[:, head : head + 1] + shut)
            weights = decay * similar
            grad_half = half_tile(grad_y_low[:, span], half)
            term = mm(weights.astype(bf16), grad_half)
            total = term if total is None else total + term
            grad_decayed = mm(stepped_low[:, span], grad_half, NT)
            grad_similar += grad_decayed * decay
            product = grad_decayed * weights
            from_source = jnp.where(lane == head, jnp.sum(product, axis=1, keepdims=True), from_source)
            target_rows.append(jnp.sum(product, axis=0, keepdims=True))
        tiles.append(total)
    target_rows.append(jnp.zeros((LANES - heads, length), f32))
    from_target = jnp.transpose(jnp.concatenate(target_rows, axis=0))
    grad_similar_low = grad_similar.astype(bf16)
    grad_write += mm(grad_similar_low, read)
    grad_read += mm(grad_similar_low, write, TN)
    grad_stepped = jnp.concatenate(tiles, axis=1) + back_wide * carried

    grad_cumlog = from_entry - from_back + from_target - from_source
    upper = (places <= others).astype(bf16)
    grad_log = unpack(mm(upper, pack(grad_cumlog, heads)))
    grad_log += jnp.sum(from_back, axis=0, keepdims=True) + overlap
    grad_log = jnp.where(lane < heads, grad_log, 0.0)
    grad_step = sum_heads(grad_stepped * values, collect[...]) + neg_rate * grad_log
    grad_rawstep = grad_step * sigmoid(raw_step + step_bias)
    small[5:6, model : model + LANES] += jnp.sum(grad_rawstep, axis=0, keepdims=True)
    small[5:6, model + LANES : model + 2 * LANES] += jnp.sum(grad_log * logdecay, axis=0, keepdims=True)
    skipped = jnp.sum(grad_y * values, axis=0, keepdims=True)
    small[6:7, width : width + LANES] += sum_heads(jnp.broadcast_to(skipped, (8, width)), collect[...])[0:1, :]
    grad_values = grad_stepped * step_wide + skip * grad_y
    grad_pre = jnp.concatenate([grad_values, grad_write, grad_read], axis=1) * (
        pre_sig * (1.0 + pre * (1.0 - pre_sig))
    )
    halo[0:length, :] = grad_pre
    mixer = raw_in[:, width : width + mixed_width]
    grad_mixer = grad_pre * taps[TAPS - 1 : TAPS, :]

    def add_taps(place, values):
        small[place : place + 1, :] += jnp.sum(values, axis=0, keepdims=True)

    add_taps(TAPS - 1, grad_pre * mixer)
    add_taps(TAPS, grad_pre)
    for offset in range(1, TAPS):
        place = TAPS - 1 - offset
        moved = halo[offset : offset + length, :] * masks[:, 3 + offset : 4 + offset]
        grad_mixer += moved * taps[place : place + 1, :]
        add_taps(place, moved * mixer)
    halo[length : length + HALO, :] = halo[0:HALO, :]
    halo_out[...] = halo[0:HALO, :]
    main_back = jnp.concatenate(
        [grad_z.astype(bf16), grad_mixer[:, :width].astype(bf16)], axis=1
    )
    state_back = grad_mixer[:, width:].astype(bf16)
    step_back = grad_rawstep.astype(bf16)
    joined_out[:, : 2 * width] = main_back
    joined_out[:, 2 * width : width + mixed_width] = state_back
    joined_out[:, width + mixed_width : width + mixed_width + LANES] = step_back
    spare = joined_out.shape[1] - width - mixed_width - LANES
    if spare:
        joined_out[:, width + mixed_width + LANES :] = jnp.zeros((length, spare), bf16)

    @pl.when(step_index == 0)
    def _():
        fetch.wait()

    grad_input = mm(main_back, wmain[...], NT)
    grad_input += mm(state_back, wstate[...], NT) + mm(step_back, wstep[...], NT)
    data = tokens[...].astype(f32)
    scale = norm_scale(data)
    small[5:6, :model] += jnp.sum(grad_input * data * scale, axis=0, keepdims=True)
    gained = grad_input * norm_gain
    back_out[...] = gained * scale - data * (
        scale * scale * scale * jnp.mean(gained * data, axis=1, keepdims=True)
    )


def after(value, *marks):
    def nothing(*refs):
        pass

    anywhere = pl.BlockSpec(memory_space=pl.ANY)
    return pl.pallas_call(
        nothing,
        in_specs=[anywhere] * (1 + len(marks)),
        out_specs=anywhere,
        out_shape=jax.ShapeDtypeStruct(value.shape, value.dtype),
        input_output_aliases={0: 0},
    )(value, *marks)


def swap(values):
    return lax.ppermute(values, "tensor", [(0, 1), (1, 0)])


def local(
    tokens,
    segment_ids,
    norm_gain,
    proj_main,
    proj_state,
    proj_step,
    conv_main,
    conv_state,
    bias_main,
    bias_state,
    step_bias,
    log_rate,
    skip_gain,
    gate_gain,
    out_proj,
    cotangent,
):
    packs, length, model = tokens.shape
    width = proj_main.shape[2]
    heads = step_bias.shape[0]
    state_cols = proj_state.shape[1]
    mixed_width = width + state_cols
    wall_cols = width + mixed_width + LANES
    chunk = min(CHUNK, length)
    count = length // chunk
    data = tokens.reshape(length, model)
    cot = cotangent.reshape(length, model)
    wmain = proj_main.reshape(model, 2 * width)
    wstep = jnp.pad(proj_step, ((0, 0), (0, LANES - heads)))
    taps = jnp.concatenate([conv_main, conv_state], axis=1)
    tap_bias = jnp.concatenate([bias_main, bias_state]).reshape(1, mixed_width)

    def row(values):
        return jnp.pad(values.astype(f32), (0, width - values.shape[0]))

    rows = jnp.stack(
        [
            row(norm_gain), row(gate_gain), row(jnp.repeat(skip_gain, HEAD)), row(step_bias),
            row(-jnp.exp(log_rate)), row(step_bias), row(step_bias), row(step_bias),
        ]
    )
    places = np.arange(LANES)[:, None]
    owner = np.arange(width)[None, :] // HEAD
    expand = jnp.asarray((places % 16 == owner) & (places < 48), bf16)
    collect = jnp.asarray((places == owner).T, bf16)
    anywhere = pl.BlockSpec(memory_space=pl.ANY)
    scalars = pl.BlockSpec(memory_space=pltpu.SMEM)

    def whole(shape):
        return pl.BlockSpec(shape, lambda i: (0,) * len(shape))

    def shaped(*members):
        return [jax.ShapeDtypeStruct(shape, kind) for shape, kind in members]

    def block(cols, first):
        return pl.BlockSpec((chunk, cols), lambda i: (first + i, 0))

    def wide(count_rows, first):
        return pl.BlockSpec((count_rows, chunk), lambda i: (0, first + i))

    def states(first):
        return pl.BlockSpec((1, STATE, width), lambda i: (first + i, 0, 0))

    params = pltpu.CompilerParams(
        dimension_semantics=("arbitrary",), vmem_limit_bytes=VMEM_BYTES
    )

    def forward(first, spans, kept, carried):
        steps = spans[-1] // chunk
        pieces = [high - low for low, high in zip((0, *spans), spans)]
        return pl.pallas_call(
            lambda *refs: forward_kernel(heads, first, len(kept), spans, *refs),
            grid=(steps,),
            in_specs=[
                block(model, first), whole((1, length)), scalars, block(model, first),
                whole((8, width)), whole((model, 2 * width)), whole((model, state_cols)),
                whole((model, LANES)), whole((TAPS, mixed_width)), whole((1, mixed_width)),
                whole((width, model)), whole((LANES, width)),
                *[whole(member.shape) for member in carried], *[anywhere] * len(kept),
            ],
            out_specs=[
                block(model, first), block(wall_cols, first), block(mixed_width, first),
                block(width, first), block(width, first), wide(8, first), states(first),
                whole((STATE, width)), whole((HALO, mixed_width)),
                *[whole((piece, model)) for piece in pieces],
            ],
            out_shape=shaped(
                ((length, model), bf16), ((length, wall_cols), f32),
                ((length, mixed_width), f32), ((length, width), f32), ((length, width), bf16),
                ((8, length), f32), ((count, STATE, width), f32), ((STATE, width), f32),
                ((HALO, mixed_width), f32), *[((piece, model), f32) for piece in pieces],
            ),
            scratch_shapes=[
                pltpu.VMEM((chunk + HALO, mixed_width), f32),
                pltpu.VMEM((8, length), f32),
            ],
            input_output_aliases={14 + k: k for k in range(len(kept))},
            compiler_params=params,
            cost_estimate=pl.CostEstimate(
                flops=8_000_000_000 * steps, bytes_accessed=8_000_000 * steps,
                transcendentals=0,
            ),
        )(data, segment_ids, segment_ids, cot, rows, wmain, proj_state, wstep, taps, tap_bias,
          out_proj, expand, *carried, *kept)

    begun = forward(0, (chunk,), (), ())
    partials = list(begun[9:])
    others = [swap(partials[0])]
    rest = length - chunk
    begun = forward(1, (rest // 2, rest), begun[:7], begun[7:9])
    partials += begun[9:]
    normed, raw, pre, y, scaled, stats, entries = begun[:7]
    stats = after(stats, others[0])
    totals = stats[:2] + swap(stats[:2])
    rscale = lax.rsqrt(totals[0] / INNER + epsilon)
    ratio = totals[1] * rscale * rscale * rscale
    scales = jnp.pad(jnp.stack([rscale, ratio]), ((0, 6), (0, 0)))
    for piece in (1, 2):
        partials[piece] = after(partials[piece], others[piece - 1])
        others.append(swap(partials[piece]))
    joined_cols = wall_cols + -wall_cols % (2 * LANES)

    def backward(place, steps, resumed, marks):
        def block(cols):
            return pl.BlockSpec((chunk, cols), lambda i: (place - i, 0))

        return pl.pallas_call(
            lambda *refs: backward_kernel(heads, place, len(resumed) > 0, len(marks), *refs),
            grid=(steps,),
            in_specs=[
                block(model), whole((1, length)), scalars, block(model),
                whole((8, width)), anywhere, whole((model, state_cols)),
                whole((model, LANES)), whole((TAPS, mixed_width)), whole((width, model)),
                whole((LANES, width)), whole((width, LANES)),
                block(wall_cols), block(mixed_width), block(width),
                pl.BlockSpec((8, chunk), lambda i: (0, place - i)),
                pl.BlockSpec((1, STATE, width), lambda i: (place - i, 0, 0)),
                *[whole(member.shape) for member in resumed[1:]],
                *[anywhere] * len(resumed[:1]), *[anywhere] * len(marks),
            ],
            out_specs=[
                block(joined_cols),
                pl.BlockSpec((chunk, model), lambda i: (steps - 1 - i, 0)),
                whole((STATE, width)), whole((HALO, mixed_width)),
                whole((8, mixed_width)),
            ],
            out_shape=shaped(
                ((length, joined_cols), bf16), ((steps * chunk, model), f32),
                ((STATE, width), f32), ((HALO, mixed_width), f32),
                ((8, mixed_width), f32),
            ),
            scratch_shapes=[
                pltpu.VMEM((chunk + HALO, mixed_width), f32),
                pltpu.VMEM((8, length), f32),
                pltpu.VMEM((model, 2 * width), bf16),
                pltpu.SemaphoreType.DMA,
            ],
            input_output_aliases={20 + k: k for k in range(len(resumed[:1]))},
            compiler_params=params,
            cost_estimate=pl.CostEstimate(
                flops=12_000_000_000 * steps, bytes_accessed=10_000_000 * steps,
                transcendentals=0,
            ),
        )(data, segment_ids, segment_ids, cot, rows, wmain, proj_state, wstep, taps, out_proj,
          expand, collect, raw, pre, y, scales, entries, *resumed[1:], *resumed[:1], *marks)

    grad_part = (rscale[:, None] * cot.astype(f32)).astype(bf16)
    outproj_sum = GroupedSum(mm(grad_part, scaled, TN))
    half = count // 2
    done = backward(count - 1, count - half, (), ())
    back_late = done[1]
    outproj_sum.ring("core")
    outproj_sum.total = after(outproj_sum.total, back_late)
    outproj_sum.ring("y")
    marks = (others[1],)
    done = backward(half - 1, half, (done[0], *done[2:]), marks)
    joined, back_early, _, _, small = done
    joined = after(joined, others[2], outproj_sum.total)
    over_tensor = np.zeros((8, mixed_width), bool)
    over_tensor[:TAPS + 1, width:] = True
    over_tensor[TAPS + 1, :model] = True
    small = small + jnp.where(over_tensor, swap(small), 0.0)
    back_late = after(back_late, others[2], small)
    back_early = after(back_early, small)
    late_other = swap(back_late)
    early_other = swap(back_early)

    wall_sum = ScatterSum(normed, joined, "yx", small)
    wall_sum.send()
    outproj_sum.total = after(outproj_sum.total, wall_sum.parts[1])
    outproj_sum.ring("x")
    wall_sum.receive(late_other)
    late_other = after(late_other, wall_sum.total)
    others = [after(other, wall_sum.total) for other in others]
    wall_sum.send()
    wall_sum.receive(outproj_sum.total)
    wall_sum.widen(outproj_sum.total)
    wall_sum.order = ["z"] if "z" in wall_sum.rings else []
    wall_sum.send()
    wall_sum.receive(early_other)
    early_other = after(early_other, wall_sum.total)
    reduced, summed = wall_sum.finish()
    wall_half = joined_cols // 2
    grad_outproj = jnp.concatenate(
        [reduced[0, :, wall_half:], reduced[1, :, wall_half:]], axis=1
    )
    reduced = jnp.concatenate([reduced[0, :, :wall_half], reduced[1, :, :wall_half]], axis=1)
    grad_state = reduced[:, 2 * width : width + mixed_width]
    grad_state = grad_state + swap(grad_state)
    grad_tokens = (
        cot.astype(f32)
        + jnp.concatenate([back_early + early_other, back_late + late_other])
    ).astype(bf16)
    mixed = (
        data.astype(f32)
        + rscale[:, None]
        * jnp.concatenate([mine + other for mine, other in zip(partials, others)])
    ).astype(bf16)

    return (
        mixed.reshape(tokens.shape),
        grad_tokens.reshape(tokens.shape),
        summed[5, :model],
        reduced[:, : 2 * width].reshape(-1, 2, width),
        grad_state,
        reduced[:, width + mixed_width : width + mixed_width + heads],
        summed[:TAPS, :width],
        summed[:TAPS, width:mixed_width],
        summed[TAPS, :width],
        summed[TAPS, width:mixed_width],
        summed[5, model : model + heads],
        summed[5, model + LANES : model + LANES + heads],
        summed[6, width : width + heads],
        summed[6, :width],
        grad_outproj.T,
    )


RINGS = (("y", 4), ("z", 2), ("x", 4), ("core", 2))


def ring_place(index, ring):
    for name, size in reversed(RINGS):
        if name == ring:
            return index % size
        index = index // size


def ring_shift(values, ring, step):
    pairs = []
    for source in range(math.prod(size for _, size in RINGS)):
        stride = 1
        for name, size in reversed(RINGS):
            if name == ring:
                place = source // stride % size
                pairs.append((source, source + ((place + step) % size - place) * stride))
            stride *= size
    return lax.ppermute(values, "dp", pairs)


class ScatterSum:

    def __init__(self, left, right, order, extra):
        self.index = lax.axis_index("dp")
        self.core = ring_place(self.index, "core")
        self.order = list(order)
        half = right.shape[1] // 2

        def product(which):
            return mm(left, lax.dynamic_slice_in_dim(right, which * half, half, axis=1), TN)

        away = ring_shift(product(1 - self.core), "core", 1)
        self.total = product(self.core) + away
        self.extra = extra + ring_shift(extra, "core", 1)
        self.rings = [name for name, _ in RINGS if name != "core"]

    def send(self):
        self.moved = []
        if not self.order:
            self.parts = [self.total] * 2
            return
        ring = self.order.pop(0)
        sizes = dict(RINGS)
        axis, size = self.rings.index(ring), sizes[ring]
        spans = [sizes[name] for name in self.rings]
        rows, cols = self.total.shape
        split = self.total.reshape(spans + [rows // math.prod(spans), cols])
        place = ring_place(self.index, ring)
        self.parts = [
            jnp.concatenate(
                [
                    lax.dynamic_index_in_dim(
                        split, (place + step) % size, axis, keepdims=False
                    ).reshape(rows // size, cols),
                    self.extra,
                ]
            )
            for step in range(size)
        ]
        self.moved = [ring_shift(self.parts[step], ring, step) for step in range(1, size)]
        self.rings.remove(ring)

    def receive(self, *marks):
        if not self.moved:
            return
        total = self.parts[0]
        if marks:
            total = after(total, *marks)
        for member in self.moved:
            total = total + member
        rows = total.shape[0] - self.extra.shape[0]
        self.total, self.extra = total[:rows], total[rows:]

    def widen(self, columns):
        self.total = jnp.concatenate([self.total, columns], axis=1)
        self.extra = jnp.pad(self.extra, ((0, 0), (0, columns.shape[1])))

    def finish(self):
        core, total = self.core, self.total
        share = total.shape[0] // 2
        mine = lax.dynamic_slice_in_dim(total, core * share, share, axis=0)
        other = lax.dynamic_slice_in_dim(total, (1 - core) * share, share, axis=0)
        other = ring_shift(other, "core", 1)
        halves = jnp.where(core == 0, jnp.stack([mine, other]), jnp.stack([other, mine]))
        return halves, self.extra


class GroupedSum:

    def __init__(self, product):
        rows, cols = product.shape
        self.core = ring_place(lax.axis_index("dp"), "core")
        self.total = product.reshape(rows, 2, cols // 2).transpose(1, 0, 2)

    def ring(self, ring):
        stride, size = 1, 1
        for name, size in reversed(RINGS):
            if name == ring:
                break
            stride *= size
        if name != ring:
            return
        devices = math.prod(size for _, size in RINGS)
        groups = [
            [start + place * stride for place in range(size)]
            for start in range(devices)
            if start // stride % size == 0
        ]
        if ring != "core":
            rows, cols = self.total.shape
            if ring == "x":
                total = self.total.reshape(rows // (24 * size), size, 24, cols)
                self.total = total.transpose(1, 0, 2, 3).reshape(size, rows // size, cols)
            else:
                self.total = self.total.reshape(size, rows // size, cols)
        self.total = lax.psum_scatter(
            self.total, "dp", scatter_dimension=0, axis_index_groups=groups, tiled=False
        )


def solution(mesh):
    placed = (
        P("dp", None, None),
        P("dp", None),
        P(),
        P(None, None, "tensor"),
        P(),
        P(None, "tensor"),
        P(None, "tensor"),
        P(),
        P("tensor"),
        P(),
        P("tensor"),
        P("tensor"),
        P("tensor"),
        P("tensor"),
        P("tensor", None),
        P("dp", None, None),
    )
    return jax.shard_map(
        local,
        mesh=mesh,
        in_specs=placed,
        out_specs=(
            P("dp", None, None),
            P("dp", None, None),
            P(),
            P("dp", None, "tensor"),
            P("dp", None),
            P("dp", "tensor"),
            P(None, "tensor"),
            P(),
            P("tensor"),
            P(),
            P("tensor"),
            P("tensor"),
            P("tensor"),
            P("tensor"),
            P("tensor", "dp"),
        ),
        check_vma=False,
    )
```

```python
import math

import jax
import jax.numpy as jnp
import numpy as np
from jax import lax
from jax.experimental import pallas as pl
from jax.experimental.pallas import tpu as pltpu
from jax.sharding import PartitionSpec as P

INNER = 1536
TAPS = 4
LANES = 128
HEAD = 64
STATE = 128
CHUNK = 256
HALO = 8
VMEM_BYTES = 56 * 1024 * 1024

epsilon = 1e-05
f32 = jnp.float32
bf16 = jnp.bfloat16

NN = ((1,), (0,))
NT = ((1,), (1,))
TN = ((0,), (0,))


def mm(left, right, dims=NN):
    return lax.dot_general(left, right, (dims, ((), ())), preferred_element_type=f32)


def lane_iota(shape):
    return lax.broadcasted_iota(jnp.int32, shape, 1)


def pack(values, heads):
    values = jnp.where(lane_iota(values.shape) < heads, values, 0.0)
    high = values.astype(bf16).astype(f32)
    rest = values - high
    middle = rest.astype(bf16).astype(f32)
    low = (rest - middle).astype(bf16).astype(f32)
    return (high + pltpu.roll(middle, 16, 1) + pltpu.roll(low, 32, 1)).astype(bf16)


def unpack(values):
    return values + pltpu.roll(values, LANES - 16, 1) + pltpu.roll(values, LANES - 32, 1)


def spread_heads(values, expand, heads):
    return mm(pack(values, heads), expand)


def sum_heads(values, collect):
    high = values.astype(bf16)
    low = (values - high.astype(f32)).astype(bf16)
    return mm(high, collect) + mm(low, collect)


def sigmoid(values):
    return 1.0 / (1.0 + jnp.exp(-values))


def softplus(values):
    return jnp.maximum(values, 0.0) + jnp.log1p(jnp.exp(-jnp.abs(values)))


def half_tile(values, half):
    lane = lane_iota(values.shape)
    keep = lane < HEAD if half == 0 else lane >= HEAD
    return jnp.where(keep, values, jnp.zeros_like(values))


def norm_scale(data):
    return lax.rsqrt(jnp.mean(data * data, axis=1, keepdims=True) + epsilon)


def scan_sizes(raw_step, step_bias, neg_rate, from_prior, to_last, heads, length):
    step = softplus(raw_step + step_bias)
    logdecay = step * neg_rate
    places = lax.broadcasted_iota(jnp.int32, (length, length), 0)
    others = lax.broadcasted_iota(jnp.int32, (length, length), 1)
    lower = (places >= others).astype(bf16)
    cumlog = unpack(mm(lower, pack(logdecay, heads)))
    entry = from_prior * jnp.exp(cumlog)
    back = to_last * jnp.exp(cumlog[length - 1 : length] - cumlog)
    return step, logdecay, cumlog, entry, back


def segment_columns(seg_row, seg_scalar, rows, place, length):
    total = seg_row.shape[1]
    full = jnp.broadcast_to(seg_row[...].astype(f32), (8, total))
    lane = lane_iota((8, total))
    sub = lax.broadcasted_iota(jnp.int32, (8, total), 0)
    table = full
    for offset in range(1, TAPS):
        before = (pltpu.roll(full, offset, 1) == full) & (lane >= offset)
        after = (pltpu.roll(full, total - offset, 1) == full) & (lane < total - offset)
        table = jnp.where(sub == offset, jnp.where(before, 1.0, 0.0), table)
        table = jnp.where(sub == TAPS - 1 + offset, jnp.where(after, 1.0, 0.0), table)
    rows[...] = table
    start = pl.multiple_of(place * length, length)
    here = rows[:, pl.ds(start, length)]
    columns = jnp.transpose(
        jnp.concatenate([here, jnp.zeros((LANES - 8, length), f32)], axis=0)
    )
    prior = jnp.where(place == 0, -1, seg_scalar[0, jnp.maximum(start - 1, 0)]).astype(f32)
    last = seg_scalar[0, start + length - 1].astype(f32)
    own = columns[:, 0:1]
    from_prior = jnp.where(own == prior, 1.0, 0.0)
    to_last = jnp.where(own == last, 1.0, 0.0)
    return columns, here[0:1, :], from_prior, to_last


def forward_kernel(heads, first, kept, spans, *refs):
    (tokens, seg_row, seg_scalar, cotangent, gains, per_head, wmain, wstate, wstep, taps,
     tap_bias, out_proj, expand) = refs[:13]
    refs = refs[13:]
    if first:
        state_in, halo_in = refs[:2]
        refs = refs[2 + kept :]
    (normed_out, gate_out, raw_out, pre_out, y_out, scaled_out, stats_out, state_out,
     state, halo_out) = refs[:10]
    partial_outs = refs[10:-2]
    halo, seg_rows = refs[-2:]
    norm_gain, gate_gain = gains[0:1, :], gains[1:2, :]
    step_bias, neg_rate = per_head[0:1, :], -jnp.exp(per_head[1:2, :])
    skip = spread_heads(per_head[...], expand[...], heads)[2:3, :]
    length = tokens.shape[0]
    width = wmain.shape[1] // 2
    mixed_width = width + 2 * STATE
    step_index = pl.program_id(0)

    @pl.when(step_index == 0)
    def _():
        if first:
            state[...] = state_in[...]
            halo[0:HALO, :] = halo_in[...]
        else:
            state[...] = jnp.zeros_like(state)
            halo[0:HALO, :] = jnp.zeros((HALO, mixed_width), f32)

    masks, seg_here, from_prior, to_last = segment_columns(
        seg_row, seg_scalar, seg_rows, step_index + first, length
    )
    data = tokens[...].astype(f32)
    normed = (data * norm_scale(data) * norm_gain).astype(bf16)
    normed_out[...] = normed
    raw_main = mm(normed, wmain[...])
    mixer = jnp.concatenate([raw_main[:, width:], mm(normed, wstate[...])], axis=1)
    raw_step = mm(normed, wstep[...])
    gate_out[...] = raw_main[:, :width]
    raw_out[:, :mixed_width] = mixer
    raw_out[:, mixed_width:] = raw_step
    halo[HALO : HALO + length, :] = mixer
    pre = tap_bias[...] + mixer * taps[TAPS - 1 : TAPS, :]
    for offset in range(1, TAPS):
        moved = halo[HALO - offset : HALO - offset + length, :]
        pre += moved * taps[TAPS - 1 - offset : TAPS - offset, :] * masks[:, offset : offset + 1]
    halo[0:HALO, :] = halo[length : length + HALO, :]
    halo_out[...] = halo[0:HALO, :]
    pre_out[...] = pre
    act = pre * sigmoid(pre)
    values = act[:, :width]
    write = act[:, width : width + STATE].astype(bf16)
    read = act[:, width + STATE :].astype(bf16)
    step, _, cumlog, entry, back = scan_sizes(
        raw_step, step_bias, neg_rate, from_prior, to_last, heads, length
    )
    entry_wide = spread_heads(entry, expand[...], heads)
    back_wide = spread_heads(back, expand[...], heads)
    stepped = values * spread_heads(step, expand[...], heads)
    before = state[...]
    state_out[0] = before
    across = mm(read, before.astype(bf16)) * entry_wide
    state[...] = before * entry_wide[length - 1 : length, :] + mm(
        write, (stepped * back_wide).astype(bf16), TN
    )
    similar = mm(read, write, NT)
    places = lax.broadcasted_iota(jnp.int32, (length, length), 0)
    others = lax.broadcasted_iota(jnp.int32, (length, length), 1)
    open_pair = (masks[:, 0:1] == seg_here) & (places >= others)
    shut = jnp.where(open_pair, 0.0, -1e30)
    cum_rows = jnp.transpose(cumlog)
    stepped_low = stepped.astype(bf16)
    tiles = []
    for pair in range(heads // 2):
        tile = stepped_low[:, pair * LANES : (pair + 1) * LANES]
        total = None
        for half in range(2):
            head = 2 * pair + half
            decay = jnp.exp(cumlog[:, head : head + 1] - cum_rows[head : head + 1, :] + shut)
            term = mm((decay * similar).astype(bf16), half_tile(tile, half))
            total = term if total is None else total + term
        tiles.append(total)
    y = jnp.concatenate(tiles, axis=1) + across + skip * values
    y_out[...] = y
    gate = raw_main[:, :width]
    gated = y * (gate * sigmoid(gate))
    squares = jnp.sum(gated * gated, axis=1, keepdims=True)
    scaled = (gated * gate_gain).astype(bf16)
    scaled_out[...] = scaled
    partial = mm(scaled, out_proj[...])
    for order in range(spans[-1] // length):

        @pl.when(step_index == order)
        def _(begin=order * length):
            low = 0
            for high, partial_out in zip(spans, partial_outs):
                left, right = max(low, begin), min(high, begin + length)
                if left < right:
                    partial_out[left - low : right - low, :] = partial[left - begin : right - begin]
                low = high

    along = jnp.sum(cotangent[...].astype(f32) * partial, axis=1, keepdims=True)
    lane = lane_iota((length, LANES))
    stats = jnp.where(lane == 0, squares, jnp.where(lane == 1, along, 0.0))
    stats_out[...] = jnp.transpose(stats)[0:8, :]


def gate_kernel(groups, cotangent, gate_in, y_in, scales, gains, out_proj, normed, scaled,
                grad_y_out, grad_z_out, products, grad_gate):
    length = cotangent.shape[0]

    @pl.when(pl.program_id(0) == 0)
    def _():
        products[...] = jnp.zeros_like(products)
        grad_gate[...] = jnp.zeros_like(grad_gate)

    zeros = jnp.zeros((LANES - 8, length), f32)
    columns = jnp.transpose(jnp.concatenate([scales[...], zeros], 0))
    rscale = columns[:, 0:1]
    ratio = columns[:, 1:2]
    grad_part = (rscale * cotangent[...].astype(f32)).astype(bf16)
    grad_scaled = mm(grad_part, out_proj[...], NT)
    gate = gate_in[...]
    gate_sig = sigmoid(gate)
    gate_silu = gate * gate_sig
    y = y_in[...]
    gated = y * gate_silu
    grad_gate[0:1, :] += jnp.sum(grad_scaled * gated, axis=0, keepdims=True)
    grad_gated = grad_scaled * gains[1:2, :] - ratio * gated * (1.0 / INNER)
    grad_y_out[...] = grad_gated * gate_silu
    grad_z = (grad_gated * y * (gate_sig * (1.0 + gate * (1.0 - gate_sig)))).astype(bf16)
    grad_z_out[...] = grad_z
    for which, (left, right) in enumerate(((normed[...], grad_z), (grad_part, scaled[...]))):
        product = mm(left, right, TN)
        span = product.shape[0] // len(groups)
        for place, source in enumerate(groups):
            products[which, place * span : (place + 1) * span, :] += product[
                source * span : (source + 1) * span
            ]


def backward_kernel(heads, place, resumed, marks, *refs):
    (tokens, seg_row, seg_scalar, gains, per_head, wmain_far, wstate, wstep, taps,
     expand, collect, raw_in, pre_in, grad_y_in, grad_z_in, state_in, gate_sums) = refs[:17]
    refs = refs[17:]
    if resumed:
        state_grad_in, halo_in, small_in = refs[:3]
        refs = refs[4:]
    refs = refs[marks:]
    (joined_out, back_out, state_grad, halo_out, small,
     halo, seg_rows, wmain, arrived) = refs
    norm_gain = gains[0:1, :]
    step_bias, neg_rate = per_head[0:1, :], -jnp.exp(per_head[1:2, :])
    skip = spread_heads(per_head[...], expand[...], heads)[2:3, :]
    length = tokens.shape[0]
    width = wmain.shape[1] // 2
    model = tokens.shape[1]
    mixed_width = width + 2 * STATE
    fetch = pltpu.make_async_copy(wmain_far, wmain, arrived)
    step_index = pl.program_id(0)

    @pl.when(step_index == 0)
    def _():
        fetch.start()
        if resumed:
            state_grad[...] = state_grad_in[...]
            halo[length : length + HALO, :] = halo_in[...]
            small[...] = small_in[...]
        else:
            halo[length : length + HALO, :] = jnp.zeros((HALO, mixed_width), f32)
            for member in (state_grad, small):
                member[...] = jnp.zeros_like(member)
            small[6:7, :width] = gate_sums[0:1, :]

    masks, seg_here, from_prior, to_last = segment_columns(
        seg_row, seg_scalar, seg_rows, place - step_index, length
    )
    grad_y = grad_y_in[...]
    grad_z = grad_z_in[...]
    pre = pre_in[...]
    pre_sig = sigmoid(pre)
    act = pre * pre_sig
    values = act[:, :width]
    write = act[:, width : width + STATE].astype(bf16)
    read = act[:, width + STATE :].astype(bf16)
    raw_step = raw_in[:, mixed_width:]
    step, logdecay, cumlog, entry, back = scan_sizes(
        raw_step, step_bias, neg_rate, from_prior, to_last, heads, length
    )
    entry_wide = spread_heads(entry, expand[...], heads)
    back_wide = spread_heads(back, expand[...], heads)
    step_wide = spread_heads(step, expand[...], heads)
    stepped = values * step_wide
    before = state_in[0]
    before_low = before.astype(bf16)
    after_grad = state_grad[...]
    after_low = after_grad.astype(bf16)
    grad_entry = grad_y * entry_wide
    grad_entry_low = grad_entry.astype(bf16)
    grad_y_low = grad_y.astype(bf16)
    stepped_low = stepped.astype(bf16)
    stepped_back = stepped * back_wide
    from_entry = sum_heads(grad_entry * mm(read, before_low), collect[...])
    grad_read = mm(grad_entry_low, before_low, NT)
    carried = mm(write, after_low)
    from_back = sum_heads(stepped_back * carried, collect[...])
    grad_write = mm(stepped_back.astype(bf16), after_low, NT)
    overlap = jnp.sum(before * after_grad, axis=0, keepdims=True) * entry_wide[length - 1 : length, :]
    overlap = sum_heads(jnp.broadcast_to(overlap, (8, width)), collect[...])[0:1, :]
    state_grad[...] = after_grad * entry_wide[length - 1 : length, :] + mm(read, grad_entry_low, TN)

    similar = mm(write, read, NT)
    places = lax.broadcasted_iota(jnp.int32, (length, length), 0)
    others = lax.broadcasted_iota(jnp.int32, (length, length), 1)
    open_pair = (masks[:, 0:1] == seg_here) & (places <= others)
    shut = jnp.where(open_pair, 0.0, -1e30)
    cum_rows = jnp.transpose(cumlog)
    lane = lane_iota((length, LANES))
    grad_similar = jnp.zeros((length, length), f32)
    from_source = jnp.zeros((length, LANES), f32)
    target_rows = []
    tiles = []
    for pair in range(heads // 2):
        span = slice(pair * LANES, (pair + 1) * LANES)
        total = None
        for half in range(2):
            head = 2 * pair + half
            decay = jnp.exp(cum_rows[head : head + 1, :] - cumlog[:, head : head + 1] + shut)
            weights = decay * similar
            grad_half = half_tile(grad_y_low[:, span], half)
            term = mm(weights.astype(bf16), grad_half)
            total = term if total is None else total + term
            grad_decayed = mm(stepped_low[:, span], grad_half, NT)
            grad_similar += grad_decayed * decay
            product = grad_decayed * weights
            from_source = jnp.where(lane == head, jnp.sum(product, axis=1, keepdims=True), from_source)
            target_rows.append(jnp.sum(product, axis=0, keepdims=True))
        tiles.append(total)
    target_rows.append(jnp.zeros((LANES - heads, length), f32))
    from_target = jnp.transpose(jnp.concatenate(target_rows, axis=0))
    grad_similar_low = grad_similar.astype(bf16)
    grad_write += mm(grad_similar_low, read)
    grad_read += mm(grad_similar_low, write, TN)
    grad_stepped = jnp.concatenate(tiles, axis=1) + back_wide * carried

    grad_cumlog = from_entry - from_back + from_target - from_source
    upper = (places <= others).astype(bf16)
    grad_log = unpack(mm(upper, pack(grad_cumlog, heads)))
    grad_log += jnp.sum(from_back, axis=0, keepdims=True) + overlap
    grad_log = jnp.where(lane < heads, grad_log, 0.0)
    grad_step = sum_heads(grad_stepped * values, collect[...]) + neg_rate * grad_log
    grad_rawstep = grad_step * sigmoid(raw_step + step_bias)
    small[5:6, model : model + LANES] += jnp.sum(grad_rawstep, axis=0, keepdims=True)
    small[5:6, model + LANES : model + 2 * LANES] += jnp.sum(grad_log * logdecay, axis=0, keepdims=True)
    skipped = jnp.sum(grad_y * values, axis=0, keepdims=True)
    small[6:7, width : width + LANES] += sum_heads(jnp.broadcast_to(skipped, (8, width)), collect[...])[0:1, :]
    grad_values = grad_stepped * step_wide + skip * grad_y
    grad_pre = jnp.concatenate([grad_values, grad_write, grad_read], axis=1) * (
        pre_sig * (1.0 + pre * (1.0 - pre_sig))
    )
    halo[0:length, :] = grad_pre
    mixer = raw_in[:, :mixed_width]
    grad_mixer = grad_pre * taps[TAPS - 1 : TAPS, :]

    def add_taps(place, values):
        small[place : place + 1, :] += jnp.sum(values, axis=0, keepdims=True)

    add_taps(TAPS - 1, grad_pre * mixer)
    add_taps(TAPS, grad_pre)
    for offset in range(1, TAPS):
        place = TAPS - 1 - offset
        moved = halo[offset : offset + length, :] * masks[:, 3 + offset : 4 + offset]
        grad_mixer += moved * taps[place : place + 1, :]
        add_taps(place, moved * mixer)
    halo[length : length + HALO, :] = halo[0:HALO, :]
    halo_out[...] = halo[0:HALO, :]
    main_back = jnp.concatenate(
        [grad_z, grad_mixer[:, :width].astype(bf16)], axis=1
    )
    state_back = grad_mixer[:, width:].astype(bf16)
    step_back = grad_rawstep.astype(bf16)
    joined_out[:, :width] = main_back[:, width:]
    joined_out[:, width:mixed_width] = state_back
    joined_out[:, mixed_width : mixed_width + LANES] = step_back
    spare = joined_out.shape[1] - mixed_width - LANES
    if spare:
        joined_out[:, mixed_width + LANES :] = jnp.zeros((length, spare), bf16)

    @pl.when(step_index == 0)
    def _():
        fetch.wait()

    grad_input = mm(main_back, wmain[...], NT)
    grad_input += mm(state_back, wstate[...], NT) + mm(step_back, wstep[...], NT)
    data = tokens[...].astype(f32)
    scale = norm_scale(data)
    small[5:6, :model] += jnp.sum(grad_input * data * scale, axis=0, keepdims=True)
    gained = grad_input * norm_gain
    back_out[...] = gained * scale - data * (
        scale * scale * scale * jnp.mean(gained * data, axis=1, keepdims=True)
    )


def after(value, *marks):
    def nothing(*refs):
        pass

    anywhere = pl.BlockSpec(memory_space=pl.ANY)
    return pl.pallas_call(
        nothing,
        in_specs=[anywhere] * (1 + len(marks)),
        out_specs=anywhere,
        out_shape=jax.ShapeDtypeStruct(value.shape, value.dtype),
        input_output_aliases={0: 0},
    )(value, *marks)


def swap(values):
    return lax.ppermute(values, "tensor", [(0, 1), (1, 0)])


def local(
    tokens,
    segment_ids,
    norm_gain,
    proj_main,
    proj_state,
    proj_step,
    conv_main,
    conv_state,
    bias_main,
    bias_state,
    step_bias,
    log_rate,
    skip_gain,
    gate_gain,
    out_proj,
    cotangent,
):
    packs, length, model = tokens.shape
    width = proj_main.shape[2]
    heads = step_bias.shape[0]
    state_cols = proj_state.shape[1]
    mixed_width = width + state_cols
    rest_cols = mixed_width + LANES
    chunk = min(CHUNK, length)
    count = length // chunk
    data = tokens.reshape(length, model)
    cot = cotangent.reshape(length, model)
    wmain = proj_main.reshape(model, 2 * width)
    wstep = jnp.pad(proj_step, ((0, 0), (0, LANES - heads)))
    taps = jnp.concatenate([conv_main, conv_state], axis=1)
    tap_bias = jnp.concatenate([bias_main, bias_state]).reshape(1, mixed_width)

    gains = jnp.stack([norm_gain, gate_gain]).astype(f32)
    per_head = jnp.pad(
        jnp.stack([step_bias, log_rate, skip_gain]), ((0, 5), (0, LANES - heads))
    )
    places = np.arange(LANES)[:, None]
    owner = np.arange(width)[None, :] // HEAD
    expand = jnp.asarray((places % 16 == owner) & (places < 48), bf16)
    collect = jnp.asarray((places == owner).T, bf16)
    anywhere = pl.BlockSpec(memory_space=pl.ANY)
    scalars = pl.BlockSpec(memory_space=pltpu.SMEM)

    def whole(shape):
        return pl.BlockSpec(shape, lambda i: (0,) * len(shape))

    def shaped(*members):
        return [jax.ShapeDtypeStruct(shape, kind) for shape, kind in members]

    def block(cols, first):
        return pl.BlockSpec((chunk, cols), lambda i: (first + i, 0))

    def wide(count_rows, first):
        return pl.BlockSpec((count_rows, chunk), lambda i: (0, first + i))

    def states(first):
        return pl.BlockSpec((1, STATE, width), lambda i: (first + i, 0, 0))

    params = pltpu.CompilerParams(
        dimension_semantics=("arbitrary",), vmem_limit_bytes=VMEM_BYTES
    )

    def forward(first, spans, kept, carried):
        steps = spans[-1] // chunk
        pieces = [high - low for low, high in zip((0, *spans), spans)]
        return pl.pallas_call(
            lambda *refs: forward_kernel(heads, first, len(kept), spans, *refs),
            grid=(steps,),
            in_specs=[
                block(model, first), whole((1, length)), scalars, block(model, first),
                whole((2, width)), whole((8, LANES)), whole((model, 2 * width)),
                whole((model, state_cols)),
                whole((model, LANES)), whole((TAPS, mixed_width)), whole((1, mixed_width)),
                whole((width, model)), whole((LANES, width)),
                *[whole(member.shape) for member in carried], *[anywhere] * len(kept),
            ],
            out_specs=[
                block(model, first), block(width, first), block(rest_cols, first),
                block(mixed_width, first),
                block(width, first), block(width, first), wide(8, first), states(first),
                whole((STATE, width)), whole((HALO, mixed_width)),
                *[whole((piece, model)) for piece in pieces],
            ],
            out_shape=shaped(
                ((length, model), bf16), ((length, width), f32), ((length, rest_cols), f32),
                ((length, mixed_width), f32), ((length, width), f32), ((length, width), bf16),
                ((8, length), f32), ((count, STATE, width), f32), ((STATE, width), f32),
                ((HALO, mixed_width), f32), *[((piece, model), f32) for piece in pieces],
            ),
            scratch_shapes=[
                pltpu.VMEM((chunk + HALO, mixed_width), f32),
                pltpu.VMEM((8, length), f32),
            ],
            input_output_aliases={15 + k: k for k in range(len(kept))},
            compiler_params=params,
            cost_estimate=pl.CostEstimate(
                flops=8_000_000_000 * steps, bytes_accessed=8_000_000 * steps,
                transcendentals=0,
            ),
        )(data, segment_ids, segment_ids, cot, gains, per_head, wmain, proj_state, wstep, taps, tap_bias,
          out_proj, expand, *carried, *kept)

    begun = forward(0, (chunk,), (), ())
    partials = list(begun[10:])
    others = [swap(partials[0])]
    rest = length - chunk
    begun = forward(1, tuple(range(chunk, rest + 1, chunk)), begun[:8], begun[8:10])
    partials += begun[10:]
    normed, gate, raw, pre, y, scaled, stats, entries = begun[:8]
    stats = after(stats, others[0])
    totals = stats[:2] + swap(stats[:2])
    rscale = lax.rsqrt(totals[0] / INNER + epsilon)
    ratio = totals[1] * rscale * rscale * rscale
    scales = jnp.pad(jnp.stack([rscale, ratio]), ((0, 6), (0, 0)))
    for piece in range(1, count):
        partials[piece] = after(partials[piece], others[piece - 1])
        others.append(swap(partials[piece]))
    joined_cols = rest_cols + -rest_cols % (2 * LANES)

    def backward(place, steps, resumed, marks):
        def block(cols):
            return pl.BlockSpec((chunk, cols), lambda i: (place - i, 0))

        return pl.pallas_call(
            lambda *refs: backward_kernel(heads, place, len(resumed) > 0, len(marks), *refs),
            grid=(steps,),
            in_specs=[
                block(model), whole((1, length)), scalars,
                whole((2, width)), whole((8, LANES)), anywhere, whole((model, state_cols)),
                whole((model, LANES)), whole((TAPS, mixed_width)),
                whole((LANES, width)), whole((width, LANES)),
                block(rest_cols), block(mixed_width), block(width), block(width),
                pl.BlockSpec((1, STATE, width), lambda i: (place - i, 0, 0)),
                whole((8, width)),
                *[whole(member.shape) for member in resumed[1:]],
                *[anywhere] * len(resumed[:1]), *[anywhere] * len(marks),
            ],
            out_specs=[
                block(joined_cols),
                pl.BlockSpec((chunk, model), lambda i: (steps - 1 - i, 0)),
                whole((STATE, width)), whole((HALO, mixed_width)),
                whole((8, mixed_width)),
            ],
            out_shape=shaped(
                ((length, joined_cols), bf16), ((steps * chunk, model), f32),
                ((STATE, width), f32), ((HALO, mixed_width), f32),
                ((8, mixed_width), f32),
            ),
            scratch_shapes=[
                pltpu.VMEM((chunk + HALO, mixed_width), f32),
                pltpu.VMEM((8, length), f32),
                pltpu.VMEM((model, 2 * width), bf16),
                pltpu.SemaphoreType.DMA,
            ],
            input_output_aliases={20 + k: k for k in range(len(resumed[:1]))},
            compiler_params=params,
            cost_estimate=pl.CostEstimate(
                flops=60_000_000_000 * steps, bytes_accessed=10_000_000 * steps,
                transcendentals=0,
            ),
        )(data, segment_ids, segment_ids, gains, per_head, wmain, proj_state, wstep, taps, expand, collect,
          raw, pre, grad_y, grad_z, entries, gate_sums, *resumed[1:], *resumed[:1], *marks)

    grad_y, grad_z, products, gate_sums = pl.pallas_call(
        lambda *refs: gate_kernel(grouped_order("yxz"), *refs),
        grid=(count,),
        in_specs=[
            block(model, 0), block(width, 0), block(width, 0), wide(8, 0), whole((2, width)),
            whole((width, model)), block(model, 0), block(width, 0),
        ],
        out_specs=[
            block(width, 0), block(width, 0), whole((2, model, width)), whole((8, width)),
        ],
        out_shape=shaped(
            ((length, width), f32), ((length, width), bf16), ((2, model, width), f32),
            ((8, width), f32),
        ),
        compiler_params=params,
        cost_estimate=pl.CostEstimate(
            flops=12_000_000_000, bytes_accessed=20_000_000, transcendentals=0
        ),
    )(cot, gate, y, scales, gains, out_proj, normed, scaled)
    early_sum = GroupedSum(products)

    half = count // 2
    done = backward(count - 1, count - half, (), (others[1],))
    back_late = done[1]
    early_sum.ring("core")
    early_sum.total = after(early_sum.total, back_late)
    early_sum.ring("y")
    marks = (others[2],)
    done = backward(half - 1, half, (done[0], *done[2:]), marks)
    joined, back_early, _, _, small = done
    joined = after(joined, others[3])
    back_late = after(back_late, others[3])
    back_early = after(back_early, others[3])
    late_other = swap(back_late)
    early_other = swap(back_early)

    wall_half = joined_cols // 2
    extra = jnp.concatenate(
        [
            small[:, :wall_half],
            jnp.pad(small[:, wall_half:], ((0, 0), (0, 2 * wall_half - mixed_width))),
        ]
    )
    over_tensor = np.zeros((16, wall_half), bool)
    over_tensor[8 : 9 + TAPS, width - wall_half : mixed_width - wall_half] = True
    over_tensor[TAPS + 1, :] = True
    over_tensor[9 + TAPS, : model - wall_half] = True
    wall_sum = ScatterSum(normed, joined, "yx", extra, over_tensor)
    wall_sum.send()
    early_sum.ring("x")
    wall_sum.receive(early_sum.total, late_other)
    late_other = after(late_other, wall_sum.total)
    others = [after(other, wall_sum.total) for other in others]
    wall_sum.send()
    wall_sum.receive()
    halves, extra = wall_sum.finish(
        early_sum.total, slice(width - wall_half, mixed_width - wall_half)
    )
    early_other = after(early_other, halves)
    summed = jnp.concatenate([extra[:8, :wall_half], extra[8:, : mixed_width - wall_half]], axis=1)
    grad_z_main = halves[0, :, wall_half:]
    grad_outproj = halves[1, :, wall_half:]
    reduced = jnp.concatenate([halves[0, :, :wall_half], halves[1, :, :wall_half]], axis=1)
    grad_state = reduced[:, width:mixed_width]
    grad_tokens = (
        cot.astype(f32)
        + jnp.concatenate([back_early + early_other, back_late + late_other])
    ).astype(bf16)
    mixed = (
        data.astype(f32)
        + rscale[:, None]
        * jnp.concatenate([mine + other for mine, other in zip(partials, others)])
    ).astype(bf16)

    return (
        mixed.reshape(tokens.shape),
        grad_tokens.reshape(tokens.shape),
        summed[5, :model],
        jnp.stack([grad_z_main, reduced[:, :width]], axis=1),
        grad_state,
        reduced[:, mixed_width : mixed_width + heads],
        summed[:TAPS, :width],
        summed[:TAPS, width:mixed_width],
        summed[TAPS, :width],
        summed[TAPS, width:mixed_width],
        summed[5, model : model + heads],
        summed[5, model + LANES : model + LANES + heads],
        summed[6, width : width + heads],
        summed[6, :width],
        grad_outproj.T,
    )


RINGS = (("y", 4), ("z", 2), ("x", 4), ("core", 2))


def ring_place(index, ring):
    for name, size in reversed(RINGS):
        if name == ring:
            return index % size
        index = index // size


def ring_shift(values, ring, step):
    pairs = []
    for source in range(math.prod(size for _, size in RINGS)):
        stride = 1
        for name, size in reversed(RINGS):
            if name == ring:
                place = source // stride % size
                pairs.append((source, source + ((place + step) % size - place) * stride))
            stride *= size
    return lax.ppermute(values, "dp", pairs)


class ScatterSum:

    def __init__(self, left, right, order, extra, over_tensor):
        self.index = lax.axis_index("dp")
        self.core = ring_place(self.index, "core")
        self.order = list(order)
        half = right.shape[1] // 2

        def product(which):
            return mm(left, lax.dynamic_slice_in_dim(right, which * half, half, axis=1), TN)

        away = ring_shift(product(1 - self.core), "core", 1)
        self.total = product(self.core) + away
        self.extra = extra + ring_shift(extra, "core", 1)
        self.over_tensor = over_tensor
        self.rings = [name for name, _ in RINGS if name != "core"]

    def send(self):
        self.moved = []
        if not self.order:
            self.parts = [self.total] * 2
            return
        ring = self.order.pop(0)
        sizes = dict(RINGS)
        axis, size = self.rings.index(ring), sizes[ring]
        spans = [sizes[name] for name in self.rings]
        rows, cols = self.total.shape
        split = self.total.reshape(spans + [rows // math.prod(spans), cols])
        place = ring_place(self.index, ring)
        self.parts = [
            jnp.concatenate(
                [
                    lax.dynamic_index_in_dim(
                        split, (place + step) % size, axis, keepdims=False
                    ).reshape(rows // size, cols),
                    self.extra,
                ]
            )
            for step in range(size)
        ]
        self.moved = [ring_shift(self.parts[step], ring, step) for step in range(1, size)]
        self.rings.remove(ring)

    def receive(self, *marks):
        if not self.moved:
            return
        total = self.parts[0]
        if marks:
            total = after(total, *marks)
        for member in self.moved:
            total = total + member
        rows = total.shape[0] - self.extra.shape[0]
        self.total, self.extra = total[:rows], total[rows:]

    def finish(self, columns, shared):
        core, extra = self.core, self.extra
        total = jnp.concatenate([self.total, columns], axis=1)
        rows, cols = total.shape
        spans = dict(RINGS).get("z", 1)
        share = rows // (2 * spans)
        total = total.reshape(spans, 2, share, cols)
        mine = lax.dynamic_index_in_dim(total, core, 1, keepdims=False)
        other = lax.dynamic_index_in_dim(total, 1 - core, 1, keepdims=False)
        other = ring_shift(other, "core", 1)
        pair = [jnp.where(core == 0, mine, other), jnp.where(core == 0, other, mine)]
        total = jnp.stack(pair, axis=1)
        place = ring_place(self.index, "z") if spans > 1 else 0
        near = lax.dynamic_index_in_dim(total, place, 0, keepdims=False)
        wide = jnp.zeros((share, extra.shape[1] - (shared.stop - shared.start)), f32)

        def small(part):
            return jnp.concatenate([extra, jnp.concatenate([part[1, :, shared], wide], axis=1)])

        moved = swap(small(near))
        if spans > 1:
            far = lax.dynamic_index_in_dim(total, 1 - place, 0, keepdims=False)
            moved += swap_ring_z(small(far))
            near = near + ring_shift(far, "z", 1)
            extra = extra + ring_shift(extra, "z", 1)
        extra = extra + jnp.where(self.over_tensor, moved[: extra.shape[0]], 0.0)
        gained = moved[extra.shape[0] :, : shared.stop - shared.start]
        return near + jnp.pad(
            gained[None], ((1, 0), (0, 0), (shared.start, cols - shared.stop))
        ), extra


def swap_ring_z(values):
    stride, size = 1, 1
    for name, size in reversed(RINGS):
        if name == "z":
            break
        stride *= size
    count = math.prod(size for _, size in RINGS)
    pairs = []
    for device in range(count):
        place = device // stride % size
        target = device + ((place + 1) % size - place) * stride
        pairs += [(2 * device + part, 2 * target + 1 - part) for part in range(2)]
    return lax.ppermute(values, ("dp", "tensor"), pairs)


def grouped_order(order):
    rings = [(name, size) for name, size in RINGS if name != "core"]
    grid = np.arange(math.prod(size for _, size in rings)).reshape([size for _, size in rings])
    names = [name for name, _ in rings]
    grid = grid.transpose([names.index(name) for name in order if name in names])
    return [int(member) for member in grid.reshape(-1)]


class GroupedSum:

    def __init__(self, products):
        self.total = products

    def ring(self, ring):
        stride, size = 1, 1
        for name, size in reversed(RINGS):
            if name == ring:
                break
            stride *= size
        if name != ring:
            return
        devices = math.prod(size for _, size in RINGS)
        groups = [
            [start + place * stride for place in range(size)]
            for start in range(devices)
            if start // stride % size == 0
        ]
        if ring != "core":
            rows, cols = self.total.shape
            self.total = self.total.reshape(size, rows // size, cols)
        self.total = lax.psum_scatter(
            self.total, "dp", scatter_dimension=0, axis_index_groups=groups, tiled=False
        )


def solution(mesh):
    placed = (
        P("dp", None, None),
        P("dp", None),
        P(),
        P(None, None, "tensor"),
        P(),
        P(None, "tensor"),
        P(None, "tensor"),
        P(),
        P("tensor"),
        P(),
        P("tensor"),
        P("tensor"),
        P("tensor"),
        P("tensor"),
        P("tensor", None),
        P("dp", None, None),
    )
    return jax.shard_map(
        local,
        mesh=mesh,
        in_specs=placed,
        out_specs=(
            P("dp", None, None),
            P("dp", None, None),
            P(),
            P("dp", None, "tensor"),
            P("dp", None),
            P("dp", "tensor"),
            P(None, "tensor"),
            P(),
            P("tensor"),
            P(),
            P("tensor"),
            P("tensor"),
            P("tensor"),
            P("tensor"),
            P("tensor", "dp"),
        ),
        check_vma=False,
    )
```

```python
import math

import jax
import jax.numpy as jnp
import numpy as np
from jax import lax
from jax.experimental import pallas as pl
from jax.experimental.pallas import tpu as pltpu
from jax.sharding import PartitionSpec as P

INNER = 1536
TAPS = 4
LANES = 128
HEAD = 64
STATE = 128
CHUNK = 256
HALO = 8
VMEM_BYTES = 56 * 1024 * 1024

epsilon = 1e-05
f32 = jnp.float32
bf16 = jnp.bfloat16

NN = ((1,), (0,))
NT = ((1,), (1,))
TN = ((0,), (0,))


def mm(left, right, dims=NN):
    return lax.dot_general(left, right, (dims, ((), ())), preferred_element_type=f32)


def lane_iota(shape):
    return lax.broadcasted_iota(jnp.int32, shape, 1)


def pack(values, heads):
    values = jnp.where(lane_iota(values.shape) < heads, values, 0.0)
    high = values.astype(bf16).astype(f32)
    rest = values - high
    middle = rest.astype(bf16).astype(f32)
    low = (rest - middle).astype(bf16).astype(f32)
    return (high + pltpu.roll(middle, 16, 1) + pltpu.roll(low, 32, 1)).astype(bf16)


def unpack(values):
    return values + pltpu.roll(values, LANES - 16, 1) + pltpu.roll(values, LANES - 32, 1)


def spread_heads(values, expand, heads):
    return mm(pack(values, heads), expand)


def sum_heads(values, collect):
    return mm(values.astype(bf16), collect)


def sigmoid(values):
    return 0.5 + 0.5 * jnp.tanh(0.5 * values)


def softplus(values):
    return jnp.maximum(values, 0.0) + jnp.log1p(jnp.exp(-jnp.abs(values)))


def half_tile(values, half):
    lane = lane_iota(values.shape)
    keep = lane < HEAD if half == 0 else lane >= HEAD
    return jnp.where(keep, values, jnp.zeros_like(values))


def norm_scale(data):
    return lax.rsqrt(jnp.mean(data * data, axis=1, keepdims=True) + epsilon)


def scan_sizes(raw_step, step_bias, neg_rate, from_prior, to_last, heads, length):
    step = softplus(raw_step + step_bias)
    logdecay = step * neg_rate
    places = lax.broadcasted_iota(jnp.int32, (length, length), 0)
    others = lax.broadcasted_iota(jnp.int32, (length, length), 1)
    lower = (places >= others).astype(bf16)
    cumlog = unpack(mm(lower, pack(logdecay, heads)))
    entry = from_prior * jnp.exp(cumlog)
    back = to_last * jnp.exp(cumlog[length - 1 : length] - cumlog)
    return step, logdecay, cumlog, entry, back


def segment_columns(seg_row, seg_scalar, rows, place, length):
    total = seg_row.shape[1]
    full = jnp.broadcast_to(seg_row[...].astype(f32), (8, total))
    lane = lane_iota((8, total))
    sub = lax.broadcasted_iota(jnp.int32, (8, total), 0)
    table = full
    for offset in range(1, TAPS):
        before = (pltpu.roll(full, offset, 1) == full) & (lane >= offset)
        after = (pltpu.roll(full, total - offset, 1) == full) & (lane < total - offset)
        table = jnp.where(sub == offset, jnp.where(before, 1.0, 0.0), table)
        table = jnp.where(sub == TAPS - 1 + offset, jnp.where(after, 1.0, 0.0), table)
    rows[...] = table
    start = pl.multiple_of(place * length, length)
    here = rows[:, pl.ds(start, length)]
    columns = jnp.transpose(
        jnp.concatenate([here, jnp.zeros((LANES - 8, length), f32)], axis=0)
    )
    prior = jnp.where(place == 0, -1, seg_scalar[0, jnp.maximum(start - 1, 0)]).astype(f32)
    last = seg_scalar[0, start + length - 1].astype(f32)
    own = columns[:, 0:1]
    from_prior = jnp.where(own == prior, 1.0, 0.0)
    to_last = jnp.where(own == last, 1.0, 0.0)
    return columns, here[0:1, :], from_prior, to_last


def forward_kernel(heads, first, kept, spans, *refs):
    (tokens, seg_row, seg_scalar, cotangent, gains, per_head, wmain, wstate, wstep, taps,
     tap_bias, out_proj, expand) = refs[:13]
    refs = refs[13:]
    if first:
        state_in, halo_in = refs[:2]
        refs = refs[2 + kept :]
    (normed_out, gate_out, raw_out, pre_out, y_out, scaled_out, stats_out, state_out,
     state, halo_out) = refs[:10]
    partial_outs = refs[10:-2]
    halo, seg_rows = refs[-2:]
    norm_gain, gate_gain = gains[0:1, :], gains[1:2, :]
    step_bias, neg_rate = per_head[0:1, :], -jnp.exp(per_head[1:2, :])
    skip = spread_heads(per_head[...], expand[...], heads)[2:3, :]
    length = tokens.shape[0]
    width = wmain.shape[1] // 2
    mixed_width = width + 2 * STATE
    step_index = pl.program_id(0)

    @pl.when(step_index == 0)
    def _():
        if first:
            state[...] = state_in[...]
            halo[0:HALO, :] = halo_in[...]
        else:
            state[...] = jnp.zeros_like(state)
            halo[0:HALO, :] = jnp.zeros((HALO, mixed_width), f32)

    masks, seg_here, from_prior, to_last = segment_columns(
        seg_row, seg_scalar, seg_rows, step_index + first, length
    )
    data = tokens[...].astype(f32)
    normed = (data * norm_scale(data) * norm_gain).astype(bf16)
    normed_out[...] = normed
    raw_main = mm(normed, wmain[...])
    mixer = jnp.concatenate([raw_main[:, width:], mm(normed, wstate[...])], axis=1)
    raw_step = mm(normed, wstep[...])
    gate_out[...] = raw_main[:, :width]
    raw_out[:, :mixed_width] = mixer
    raw_out[:, mixed_width:] = raw_step
    halo[HALO : HALO + length, :] = mixer
    pre = tap_bias[...] + mixer * taps[TAPS - 1 : TAPS, :]
    for offset in range(1, TAPS):
        moved = halo[HALO - offset : HALO - offset + length, :]
        pre += moved * taps[TAPS - 1 - offset : TAPS - offset, :] * masks[:, offset : offset + 1]
    halo[0:HALO, :] = halo[length : length + HALO, :]
    halo_out[...] = halo[0:HALO, :]
    pre_out[...] = pre
    act = pre * sigmoid(pre)
    values = act[:, :width]
    write = act[:, width : width + STATE].astype(bf16)
    read = act[:, width + STATE :].astype(bf16)
    step, _, cumlog, entry, back = scan_sizes(
        raw_step, step_bias, neg_rate, from_prior, to_last, heads, length
    )
    entry_wide = spread_heads(entry, expand[...], heads)
    back_wide = spread_heads(back, expand[...], heads)
    stepped = values * spread_heads(step, expand[...], heads)
    before = state[...]
    state_out[0] = before
    across = mm(read, before.astype(bf16)) * entry_wide
    state[...] = before * entry_wide[length - 1 : length, :] + mm(
        write, (stepped * back_wide).astype(bf16), TN
    )
    similar = mm(read, write, NT)
    places = lax.broadcasted_iota(jnp.int32, (length, length), 0)
    others = lax.broadcasted_iota(jnp.int32, (length, length), 1)
    open_pair = (masks[:, 0:1] == seg_here) & (places >= others)
    shut = jnp.where(open_pair, 0.0, -1e30)
    cum_rows = jnp.transpose(cumlog)
    stepped_low = stepped.astype(bf16)
    tiles = []
    for pair in range(heads // 2):
        tile = stepped_low[:, pair * LANES : (pair + 1) * LANES]
        total = None
        for half in range(2):
            head = 2 * pair + half
            decay = jnp.exp(cumlog[:, head : head + 1] - cum_rows[head : head + 1, :] + shut)
            term = mm((decay * similar).astype(bf16), half_tile(tile, half))
            total = term if total is None else total + term
        tiles.append(total)
    y = jnp.concatenate(tiles, axis=1) + across + skip * values
    y_out[...] = y
    gate = raw_main[:, :width]
    gated = y * (gate * sigmoid(gate))
    squares = jnp.sum(gated * gated, axis=1, keepdims=True)
    scaled = (gated * gate_gain).astype(bf16)
    scaled_out[...] = scaled
    partial = mm(scaled, out_proj[...])
    for order in range(spans[-1] // length):

        @pl.when(step_index == order)
        def _(begin=order * length):
            low = 0
            for high, partial_out in zip(spans, partial_outs):
                left, right = max(low, begin), min(high, begin + length)
                if left < right:
                    partial_out[left - low : right - low, :] = partial[left - begin : right - begin]
                low = high

    along = jnp.sum(cotangent[...].astype(f32) * partial, axis=1, keepdims=True)
    lane = lane_iota((length, LANES))
    stats = jnp.where(lane == 0, squares, jnp.where(lane == 1, along, 0.0))
    stats_out[...] = jnp.transpose(stats)[0:8, :]


def gate_kernel(core, cotangent, gate_in, y_in, scales, gains, out_proj, normed, scaled,
                grad_y_out, grad_z_out, kept, sent, grad_gate):
    length = cotangent.shape[0]

    @pl.when(pl.program_id(0) == 0)
    def _():
        kept[...] = jnp.zeros_like(kept)
        sent[...] = jnp.zeros_like(sent)
        grad_gate[...] = jnp.zeros_like(grad_gate)

    zeros = jnp.zeros((LANES - 8, length), f32)
    columns = jnp.transpose(jnp.concatenate([scales[...], zeros], 0))
    rscale = columns[:, 0:1]
    ratio = columns[:, 1:2]
    grad_part = (rscale * cotangent[...].astype(f32)).astype(bf16)
    grad_scaled = mm(grad_part, out_proj[...], NT)
    gate = gate_in[...]
    gate_sig = sigmoid(gate)
    gate_silu = gate * gate_sig
    y = y_in[...]
    gated = y * gate_silu
    grad_gate[0:1, :] += jnp.sum(grad_scaled * gated, axis=0, keepdims=True)
    grad_gated = grad_scaled * gains[1:2, :] - ratio * gated * (1.0 / INNER)
    grad_y_out[...] = grad_gated * gate_silu
    grad_z = (grad_gated * y * (gate_sig * (1.0 + gate * (1.0 - gate_sig)))).astype(bf16)
    grad_z_out[...] = grad_z
    first = core[0, 0] == 0
    own, part, values = normed[...], grad_part, scaled[...]
    kept[...] += mm(jnp.where(first, own, part), jnp.where(first, grad_z, values), TN)
    sent[...] += mm(jnp.where(first, part, own), jnp.where(first, values, grad_z), TN)


def backward_kernel(heads, place, steps, split, resumed, marks, *refs):
    (tokens, seg_row, seg_scalar, gains, per_head, wmain_far, wstate, wstep, taps,
     expand, collect, raw_in, pre_in, grad_y_in, grad_z_in, state_in, gate_sums) = refs[:17]
    refs = refs[17:]
    if resumed:
        state_grad_in, halo_in, small_in = refs[:3]
        refs = refs[4:]
    refs = refs[marks:]
    joined_out, state_grad, halo_out, small = refs[:4]
    back_outs = refs[4:-4]
    halo, seg_rows, wmain, arrived = refs[-4:]
    norm_gain = gains[0:1, :]
    step_bias, neg_rate = per_head[0:1, :], -jnp.exp(per_head[1:2, :])
    skip = spread_heads(per_head[...], expand[...], heads)[2:3, :]
    length = tokens.shape[0]
    width = wmain.shape[1] // 2
    model = tokens.shape[1]
    mixed_width = width + 2 * STATE
    fetch = pltpu.make_async_copy(wmain_far, wmain, arrived)
    step_index = pl.program_id(0)

    @pl.when(step_index == 0)
    def _():
        fetch.start()
        if resumed:
            state_grad[...] = state_grad_in[...]
            halo[length : length + HALO, :] = halo_in[...]
            small[...] = small_in[...]
        else:
            halo[length : length + HALO, :] = jnp.zeros((HALO, mixed_width), f32)
            for member in (state_grad, small):
                member[...] = jnp.zeros_like(member)
            small[6:7, :width] = gate_sums[0:1, :]

    masks, seg_here, from_prior, to_last = segment_columns(
        seg_row, seg_scalar, seg_rows, place - step_index, length
    )
    grad_y = grad_y_in[...]
    grad_z = grad_z_in[...]
    pre = pre_in[...]
    pre_sig = sigmoid(pre)
    act = pre * pre_sig
    values = act[:, :width]
    write = act[:, width : width + STATE].astype(bf16)
    read = act[:, width + STATE :].astype(bf16)
    raw_step = raw_in[:, mixed_width:]
    step, logdecay, cumlog, entry, back = scan_sizes(
        raw_step, step_bias, neg_rate, from_prior, to_last, heads, length
    )
    entry_wide = spread_heads(entry, expand[...], heads)
    back_wide = spread_heads(back, expand[...], heads)
    step_wide = spread_heads(step, expand[...], heads)
    stepped = values * step_wide
    before = state_in[0]
    before_low = before.astype(bf16)
    after_grad = state_grad[...]
    after_low = after_grad.astype(bf16)
    grad_entry = grad_y * entry_wide
    grad_entry_low = grad_entry.astype(bf16)
    grad_y_low = grad_y.astype(bf16)
    stepped_low = stepped.astype(bf16)
    stepped_back = stepped * back_wide
    from_entry = sum_heads(grad_entry * mm(read, before_low), collect[...])
    grad_read = mm(grad_entry_low, before_low, NT)
    carried = mm(write, after_low)
    from_back = sum_heads(stepped_back * carried, collect[...])
    grad_write = mm(stepped_back.astype(bf16), after_low, NT)
    overlap = jnp.sum(before * after_grad, axis=0, keepdims=True) * entry_wide[length - 1 : length, :]
    overlap = sum_heads(jnp.broadcast_to(overlap, (8, width)), collect[...])[0:1, :]
    state_grad[...] = after_grad * entry_wide[length - 1 : length, :] + mm(read, grad_entry_low, TN)

    similar = mm(write, read, NT)
    places = lax.broadcasted_iota(jnp.int32, (length, length), 0)
    others = lax.broadcasted_iota(jnp.int32, (length, length), 1)
    open_pair = (masks[:, 0:1] == seg_here) & (places <= others)
    shut = jnp.where(open_pair, 0.0, -1e30)
    cum_rows = jnp.transpose(cumlog)
    lane = lane_iota((length, LANES))
    grad_similar = jnp.zeros((length, length), f32)
    from_source = jnp.zeros((length, LANES), f32)
    target_rows = []
    tiles = []
    for pair in range(heads // 2):
        span = slice(pair * LANES, (pair + 1) * LANES)
        total = None
        for half in range(2):
            head = 2 * pair + half
            decay = jnp.exp(cum_rows[head : head + 1, :] - cumlog[:, head : head + 1] + shut)
            weights = decay * similar
            grad_half = half_tile(grad_y_low[:, span], half)
            term = mm(weights.astype(bf16), grad_half)
            total = term if total is None else total + term
            grad_decayed = mm(stepped_low[:, span], grad_half, NT)
            grad_similar += grad_decayed * decay
            product = grad_decayed * weights
            from_source = jnp.where(lane == head, jnp.sum(product, axis=1, keepdims=True), from_source)
            target_rows.append(jnp.sum(product, axis=0, keepdims=True))
        tiles.append(total)
    target_rows.append(jnp.zeros((LANES - heads, length), f32))
    from_target = jnp.transpose(jnp.concatenate(target_rows, axis=0))
    grad_similar_low = grad_similar.astype(bf16)
    grad_write += mm(grad_similar_low, read)
    grad_read += mm(grad_similar_low, write, TN)
    grad_stepped = jnp.concatenate(tiles, axis=1) + back_wide * carried

    grad_cumlog = from_entry - from_back + from_target - from_source
    upper = (places <= others).astype(bf16)
    grad_log = unpack(mm(upper, pack(grad_cumlog, heads)))
    grad_log += jnp.sum(from_back, axis=0, keepdims=True) + overlap
    grad_log = jnp.where(lane < heads, grad_log, 0.0)
    grad_step = sum_heads(grad_stepped * values, collect[...]) + neg_rate * grad_log
    grad_rawstep = grad_step * sigmoid(raw_step + step_bias)
    small[5:6, model : model + LANES] += jnp.sum(grad_rawstep, axis=0, keepdims=True)
    small[5:6, model + LANES : model + 2 * LANES] += jnp.sum(grad_log * logdecay, axis=0, keepdims=True)
    skipped = jnp.sum(grad_y * values, axis=0, keepdims=True)
    small[6:7, width : width + LANES] += sum_heads(jnp.broadcast_to(skipped, (8, width)), collect[...])[0:1, :]
    grad_values = grad_stepped * step_wide + skip * grad_y
    grad_pre = jnp.concatenate([grad_values, grad_write, grad_read], axis=1) * (
        pre_sig * (1.0 + pre * (1.0 - pre_sig))
    )
    halo[0:length, :] = grad_pre
    mixer = raw_in[:, :mixed_width]
    grad_mixer = grad_pre * taps[TAPS - 1 : TAPS, :]

    def add_taps(place, values):
        small[place : place + 1, :] += jnp.sum(values, axis=0, keepdims=True)

    add_taps(TAPS - 1, grad_pre * mixer)
    add_taps(TAPS, grad_pre)
    for offset in range(1, TAPS):
        place = TAPS - 1 - offset
        moved = halo[offset : offset + length, :] * masks[:, 3 + offset : 4 + offset]
        grad_mixer += moved * taps[place : place + 1, :]
        add_taps(place, moved * mixer)
    halo[length : length + HALO, :] = halo[0:HALO, :]
    halo_out[...] = halo[0:HALO, :]
    main_back = jnp.concatenate(
        [grad_z, grad_mixer[:, :width].astype(bf16)], axis=1
    )
    state_back = grad_mixer[:, width:].astype(bf16)
    step_back = grad_rawstep.astype(bf16)
    joined_out[:, :width] = main_back[:, width:]
    joined_out[:, width:mixed_width] = state_back
    joined_out[:, mixed_width : mixed_width + LANES] = step_back
    spare = joined_out.shape[1] - mixed_width - LANES
    if spare:
        joined_out[:, mixed_width + LANES :] = jnp.zeros((length, spare), bf16)

    @pl.when(step_index == 0)
    def _():
        fetch.wait()

    grad_input = mm(main_back, wmain[...], NT)
    grad_input += mm(state_back, wstate[...], NT) + mm(step_back, wstep[...], NT)
    data = tokens[...].astype(f32)
    scale = norm_scale(data)
    small[5:6, :model] += jnp.sum(grad_input * data * scale, axis=0, keepdims=True)
    gained = grad_input * norm_gain
    back = gained * scale - data * (
        scale * scale * scale * jnp.mean(gained * data, axis=1, keepdims=True)
    )
    for order in range(steps):

        @pl.when(step_index == order)
        def _(order=order):
            if split:
                back_outs[order][...] = back
            else:
                begin = (steps - 1 - order) * length
                back_outs[0][begin : begin + length, :] = back


def after(value, *marks):
    def nothing(*refs):
        pass

    anywhere = pl.BlockSpec(memory_space=pl.ANY)
    return pl.pallas_call(
        nothing,
        in_specs=[anywhere] * (1 + len(marks)),
        out_specs=anywhere,
        out_shape=jax.ShapeDtypeStruct(value.shape, value.dtype),
        input_output_aliases={0: 0},
    )(value, *marks)


def swap(values):
    return lax.ppermute(values, "tensor", [(0, 1), (1, 0)])


def local(
    tokens,
    segment_ids,
    norm_gain,
    proj_main,
    proj_state,
    proj_step,
    conv_main,
    conv_state,
    bias_main,
    bias_state,
    step_bias,
    log_rate,
    skip_gain,
    gate_gain,
    out_proj,
    cotangent,
):
    packs, length, model = tokens.shape
    width = proj_main.shape[2]
    heads = step_bias.shape[0]
    state_cols = proj_state.shape[1]
    mixed_width = width + state_cols
    rest_cols = mixed_width + LANES
    chunk = min(CHUNK, length)
    count = length // chunk
    data = tokens.reshape(length, model)
    cot = cotangent.reshape(length, model)
    wmain = proj_main.reshape(model, 2 * width)
    wstep = jnp.pad(proj_step, ((0, 0), (0, LANES - heads)))
    taps = jnp.concatenate([conv_main, conv_state], axis=1)
    tap_bias = jnp.concatenate([bias_main, bias_state]).reshape(1, mixed_width)

    gains = jnp.stack([norm_gain, gate_gain]).astype(f32)
    per_head = jnp.pad(
        jnp.stack([step_bias, log_rate, skip_gain]), ((0, 5), (0, LANES - heads))
    )
    places = np.arange(LANES)[:, None]
    owner = np.arange(width)[None, :] // HEAD
    expand = jnp.asarray((places % 16 == owner) & (places < 48), bf16)
    collect = jnp.asarray((places == owner).T, bf16)
    anywhere = pl.BlockSpec(memory_space=pl.ANY)
    scalars = pl.BlockSpec(memory_space=pltpu.SMEM)

    def whole(shape):
        return pl.BlockSpec(shape, lambda i: (0,) * len(shape))

    def shaped(*members):
        return [jax.ShapeDtypeStruct(shape, kind) for shape, kind in members]

    def block(cols, first):
        return pl.BlockSpec((chunk, cols), lambda i: (first + i, 0))

    def wide(count_rows, first):
        return pl.BlockSpec((count_rows, chunk), lambda i: (0, first + i))

    def states(first):
        return pl.BlockSpec((1, STATE, width), lambda i: (first + i, 0, 0))

    params = pltpu.CompilerParams(
        dimension_semantics=("arbitrary",), vmem_limit_bytes=VMEM_BYTES
    )

    def forward(first, spans, kept, carried):
        steps = spans[-1] // chunk
        pieces = [high - low for low, high in zip((0, *spans), spans)]
        return pl.pallas_call(
            lambda *refs: forward_kernel(heads, first, len(kept), spans, *refs),
            grid=(steps,),
            in_specs=[
                block(model, first), whole((1, length)), scalars, block(model, first),
                whole((2, width)), whole((8, LANES)), whole((model, 2 * width)),
                whole((model, state_cols)),
                whole((model, LANES)), whole((TAPS, mixed_width)), whole((1, mixed_width)),
                whole((width, model)), whole((LANES, width)),
                *[whole(member.shape) for member in carried], *[anywhere] * len(kept),
            ],
            out_specs=[
                block(model, first), block(width, first), block(rest_cols, first),
                block(mixed_width, first),
                block(width, first), block(width, first), wide(8, first), states(first),
                whole((STATE, width)), whole((HALO, mixed_width)),
                *[whole((piece, model)) for piece in pieces],
            ],
            out_shape=shaped(
                ((length, model), bf16), ((length, width), f32), ((length, rest_cols), f32),
                ((length, mixed_width), f32), ((length, width), f32), ((length, width), bf16),
                ((8, length), f32), ((count, STATE, width), f32), ((STATE, width), f32),
                ((HALO, mixed_width), f32), *[((piece, model), f32) for piece in pieces],
            ),
            scratch_shapes=[
                pltpu.VMEM((chunk + HALO, mixed_width), f32),
                pltpu.VMEM((8, length), f32),
            ],
            input_output_aliases={15 + k: k for k in range(len(kept))},
            compiler_params=params,
            cost_estimate=pl.CostEstimate(
                flops=8_000_000_000 * steps, bytes_accessed=8_000_000 * steps,
                transcendentals=0,
            ),
        )(data, segment_ids, segment_ids, cot, gains, per_head, wmain, proj_state, wstep, taps, tap_bias,
          out_proj, expand, *carried, *kept)

    begun = forward(0, (chunk,), (), ())
    partials = list(begun[10:])
    others = [swap(partials[0])]
    rest = length - chunk
    begun = forward(1, tuple(range(chunk, rest + 1, chunk)), begun[:8], begun[8:10])
    partials += begun[10:]
    normed, gate, raw, pre, y, scaled, stats, entries = begun[:8]
    stats = after(stats, others[0])
    totals = stats[:2] + swap(stats[:2])
    rscale = lax.rsqrt(totals[0] / INNER + epsilon)
    ratio = totals[1] * rscale * rscale * rscale
    scales = jnp.pad(jnp.stack([rscale, ratio]), ((0, 6), (0, 0)))
    for piece in range(1, count):
        partials[piece] = after(partials[piece], others[piece - 1])
        others.append(swap(partials[piece]))
    joined_cols = rest_cols + -rest_cols % (2 * LANES)

    def backward(place, steps, split, resumed, marks):
        pieces = [chunk] * steps if split else [steps * chunk]

        def block(cols):
            return pl.BlockSpec((chunk, cols), lambda i: (place - i, 0))

        return pl.pallas_call(
            lambda *refs: backward_kernel(
                heads, place, steps, split, len(resumed) > 0, len(marks), *refs
            ),
            grid=(steps,),
            in_specs=[
                block(model), whole((1, length)), scalars,
                whole((2, width)), whole((8, LANES)), anywhere, whole((model, state_cols)),
                whole((model, LANES)), whole((TAPS, mixed_width)),
                whole((LANES, width)), whole((width, LANES)),
                block(rest_cols), block(mixed_width), block(width), block(width),
                pl.BlockSpec((1, STATE, width), lambda i: (place - i, 0, 0)),
                whole((8, width)),
                *[whole(member.shape) for member in resumed[1:]],
                *[anywhere] * len(resumed[:1]), *[anywhere] * len(marks),
            ],
            out_specs=[
                block(joined_cols), whole((STATE, width)), whole((HALO, mixed_width)),
                whole((8, mixed_width)), *[whole((rows, model)) for rows in pieces],
            ],
            out_shape=shaped(
                ((length, joined_cols), bf16), ((STATE, width), f32),
                ((HALO, mixed_width), f32), ((8, mixed_width), f32),
                *[((rows, model), f32) for rows in pieces],
            ),
            scratch_shapes=[
                pltpu.VMEM((chunk + HALO, mixed_width), f32),
                pltpu.VMEM((8, length), f32),
                pltpu.VMEM((model, 2 * width), bf16),
                pltpu.SemaphoreType.DMA,
            ],
            input_output_aliases={20 + k: k for k in range(len(resumed[:1]))},
            compiler_params=params,
            cost_estimate=pl.CostEstimate(
                flops=60_000_000_000 * steps, bytes_accessed=10_000_000 * steps,
                transcendentals=0,
            ),
        )(data, segment_ids, segment_ids, gains, per_head, wmain, proj_state, wstep, taps, expand, collect,
          raw, pre, grad_y, grad_z, entries, gate_sums, *resumed[1:], *resumed[:1], *marks)

    core = ring_place(lax.axis_index("dp"), "core").astype(jnp.int32).reshape(1, 1)
    grad_y, grad_z, kept, sent, gate_sums = pl.pallas_call(
        gate_kernel,
        grid=(count,),
        in_specs=[
            scalars, block(model, 0), block(width, 0), block(width, 0), wide(8, 0),
            whole((2, width)),
            whole((width, model)), block(model, 0), block(width, 0),
        ],
        out_specs=[
            block(width, 0), block(width, 0), whole((model, width)), whole((model, width)),
            whole((8, width)),
        ],
        out_shape=shaped(
            ((length, width), f32), ((length, width), bf16), ((model, width), f32),
            ((model, width), f32), ((8, width), f32),
        ),
        compiler_params=params,
        cost_estimate=pl.CostEstimate(
            flops=12_000_000_000, bytes_accessed=20_000_000, transcendentals=0
        ),
    )(core, cot, gate, y, scales, gains, out_proj, normed, scaled)
    away = ring_shift(sent, "core", 1)

    half = count // 2
    done = backward(count - 1, count - half, True, (), (others[1],))
    backs = list(done[4:])
    early_sum = ScatterSum(after(kept, done[1]), away, "yx")
    early_sum.send()
    marks = (others[2],)
    joined, _, _, small, back_early = backward(half - 1, half, False, done[:4], marks)
    early_sum.receive()
    backs[0] = after(backs[0], others[2])
    back_others = [swap(backs[0])]
    joined = after(joined, others[3], back_others[0], early_sum.total)
    back_early = after(back_early, back_others[0])
    early_other = swap(back_early)
    for member in range(1, len(backs)):
        backs[member] = after(backs[member], back_others[0])
        back_others.append(swap(backs[member]))

    wall_half = joined_cols // 2
    extra = jnp.concatenate(
        [
            small[:, :wall_half],
            jnp.pad(small[:, wall_half:], ((0, 0), (0, 2 * wall_half - mixed_width))),
        ]
    )
    over_tensor = np.zeros((16, wall_half), bool)
    over_tensor[8 : 9 + TAPS, width - wall_half : mixed_width - wall_half] = True
    over_tensor[TAPS + 1, :] = True
    over_tensor[9 + TAPS, : model - wall_half] = True
    wall_sum = product_sum(normed, joined, "yx", extra)
    wall_sum.send()
    early_sum.send()
    early_sum.receive(wall_sum.parts[1])
    wall_sum.receive(early_sum.total, early_other)
    early_other = after(early_other, wall_sum.total)
    others = [after(other, wall_sum.total) for other in others]
    wall_sum.send()
    wall_sum.receive()
    halves, extra = wall_sum.finish(
        early_sum.total, slice(width - wall_half, mixed_width - wall_half), over_tensor
    )
    back_others[1:] = [after(member, halves) for member in back_others[1:]]
    summed = jnp.concatenate([extra[:8, :wall_half], extra[8:, : mixed_width - wall_half]], axis=1)
    grad_z_main = halves[0, :, wall_half:]
    grad_outproj = halves[1, :, wall_half:]
    reduced = jnp.concatenate([halves[0, :, :wall_half], halves[1, :, :wall_half]], axis=1)
    grad_state = reduced[:, width:mixed_width]
    grad_tokens = (
        cot.astype(f32)
        + jnp.concatenate(
            [
                back_early + early_other,
                *[mine + other for mine, other in zip(backs[::-1], back_others[::-1])],
            ]
        )
    ).astype(bf16)
    mixed = (
        data.astype(f32)
        + rscale[:, None]
        * jnp.concatenate([mine + other for mine, other in zip(partials, others)])
    ).astype(bf16)

    return (
        mixed.reshape(tokens.shape),
        grad_tokens.reshape(tokens.shape),
        summed[5, :model],
        jnp.stack([grad_z_main, reduced[:, :width]], axis=1),
        grad_state,
        reduced[:, mixed_width : mixed_width + heads],
        summed[:TAPS, :width],
        summed[:TAPS, width:mixed_width],
        summed[TAPS, :width],
        summed[TAPS, width:mixed_width],
        summed[5, model : model + heads],
        summed[5, model + LANES : model + LANES + heads],
        summed[6, width : width + heads],
        summed[6, :width],
        grad_outproj.T,
    )


RINGS = (("y", 4), ("z", 2), ("x", 4), ("core", 2))


def ring_place(index, ring):
    for name, size in reversed(RINGS):
        if name == ring:
            return index % size
        index = index // size


def ring_shift(values, ring, step):
    pairs = []
    for source in range(math.prod(size for _, size in RINGS)):
        stride = 1
        for name, size in reversed(RINGS):
            if name == ring:
                place = source // stride % size
                pairs.append((source, source + ((place + step) % size - place) * stride))
            stride *= size
    return lax.ppermute(values, "dp", pairs)


def product_sum(left, right, order, extra):
    core = ring_place(lax.axis_index("dp"), "core")
    half = right.shape[1] // 2

    def product(which):
        return mm(left, lax.dynamic_slice_in_dim(right, which * half, half, axis=1), TN)

    away = ring_shift(product(1 - core), "core", 1)
    extra = extra + ring_shift(extra, "core", 1)
    return ScatterSum(product(core), away, order, extra)


class ScatterSum:

    def __init__(self, kept, away, order, extra=None):
        self.index = lax.axis_index("dp")
        self.core = ring_place(self.index, "core")
        self.order = list(order)
        self.total = kept + away
        self.extra = jnp.zeros((0, kept.shape[1]), f32) if extra is None else extra
        self.rings = [name for name, _ in RINGS if name != "core"]

    def send(self):
        self.moved = []
        if not self.order:
            self.parts = [self.total] * 2
            return
        ring = self.order.pop(0)
        sizes = dict(RINGS)
        axis, size = self.rings.index(ring), sizes[ring]
        spans = [sizes[name] for name in self.rings]
        rows, cols = self.total.shape
        split = self.total.reshape(spans + [rows // math.prod(spans), cols])
        place = ring_place(self.index, ring)
        self.parts = [
            jnp.concatenate(
                [
                    lax.dynamic_index_in_dim(
                        split, (place + step) % size, axis, keepdims=False
                    ).reshape(rows // size, cols),
                    *([self.extra] if self.extra.shape[0] else []),
                ]
            )
            for step in range(size)
        ]
        self.moved = [ring_shift(self.parts[step], ring, step) for step in range(1, size)]
        self.rings.remove(ring)

    def receive(self, *marks):
        if not self.moved:
            return
        total = self.parts[0]
        if marks:
            total = after(total, *marks)
        for member in self.moved:
            total = total + member
        rows = total.shape[0] - self.extra.shape[0]
        self.total, self.extra = total[:rows], total[rows:]

    def finish(self, columns, shared, over_tensor):
        core, extra = self.core, self.extra
        total = jnp.concatenate([self.total, columns], axis=1)
        rows, cols = total.shape
        spans = dict(RINGS).get("z", 1)
        share = rows // (2 * spans)
        total = total.reshape(spans, 2, share, cols)
        mine = lax.dynamic_index_in_dim(total, core, 1, keepdims=False)
        other = lax.dynamic_index_in_dim(total, 1 - core, 1, keepdims=False)
        other = ring_shift(other, "core", 1)
        pair = [jnp.where(core == 0, mine, other), jnp.where(core == 0, other, mine)]
        total = jnp.stack(pair, axis=1)
        place = ring_place(self.index, "z") if spans > 1 else 0
        near = lax.dynamic_index_in_dim(total, place, 0, keepdims=False)
        wide = jnp.zeros((share, extra.shape[1] - (shared.stop - shared.start)), f32)

        def small(part):
            return jnp.concatenate([extra, jnp.concatenate([part[1, :, shared], wide], axis=1)])

        moved = swap(small(near))
        if spans > 1:
            far = lax.dynamic_index_in_dim(total, 1 - place, 0, keepdims=False)
            moved += swap_ring_z(small(far))
            near = near + ring_shift(far, "z", 1)
            extra = extra + ring_shift(extra, "z", 1)
        extra = extra + jnp.where(over_tensor, moved[: extra.shape[0]], 0.0)
        gained = moved[extra.shape[0] :, : shared.stop - shared.start]
        return near + jnp.pad(
            gained[None], ((1, 0), (0, 0), (shared.start, cols - shared.stop))
        ), extra


def swap_ring_z(values):
    stride, size = 1, 1
    for name, size in reversed(RINGS):
        if name == "z":
            break
        stride *= size
    count = math.prod(size for _, size in RINGS)
    pairs = []
    for device in range(count):
        place = device // stride % size
        target = device + ((place + 1) % size - place) * stride
        pairs += [(2 * device + part, 2 * target + 1 - part) for part in range(2)]
    return lax.ppermute(values, ("dp", "tensor"), pairs)


def solution(mesh):
    placed = (
        P("dp", None, None),
        P("dp", None),
        P(),
        P(None, None, "tensor"),
        P(),
        P(None, "tensor"),
        P(None, "tensor"),
        P(),
        P("tensor"),
        P(),
        P("tensor"),
        P("tensor"),
        P("tensor"),
        P("tensor"),
        P("tensor", None),
        P("dp", None, None),
    )
    return jax.shard_map(
        local,
        mesh=mesh,
        in_specs=placed,
        out_specs=(
            P("dp", None, None),
            P("dp", None, None),
            P(),
            P("dp", None, "tensor"),
            P("dp", None),
            P("dp", "tensor"),
            P(None, "tensor"),
            P(),
            P("tensor"),
            P(),
            P("tensor"),
            P("tensor"),
            P("tensor"),
            P("tensor"),
            P("tensor", "dp"),
        ),
        check_vma=False,
    )
```
